768 devices in a mesh: dp: 48 (over y, z_lo), ctx: 16 (over x, z_hi, core).
Axes of the slice: x: 4, y: 8, z: 12 (z_hi: 2, z_lo: 6; z = z_hi * 6 + z_lo), core: 2. Of those that a mesh axis runs over, the one named last changes fastest.
Arguments:
- grad_tokens: bfloat16 [12288, 8192], P(('dp', 'ctx')), may hold values from -9 to 9
- pre_act: bfloat16 [5120, 12288], P('ctx', 'dp'), may hold values from -6 to 6
- w_fc1: bfloat16 [5120, 5120], P(None, 'ctx'), may hold values from -0.078125 to 0.078125
- w_fc2: bfloat16 [5120, 8192], P(None, 'ctx'), may hold values from -0.078125 to 0.078125
- patch_in: bfloat16 [12288, 5120], P(('dp', 'ctx')), may hold values from -54 to 54
- norm_gain: float32 [1280], replicated, may hold values from 0.25 to 1.75
- owner_pos: int32 [12288], P('dp'), may hold values from 0 to 255, as said below
Outputs:
- patch_grad: bfloat16 [12288, 5120], P(('dp', 'ctx'))
- gain_grad: float32 [1280], replicated
The draws below stay inside these ranges and needn't reach their ends.
Inputs may be any that keep to these rules, and one draw needn't show every extreme that they name: `owner_pos`: each group's 256 entries (g * 256 to g * 256 + 255) are a permutation of 0 to 255; entry g * 256 + o * 16 + i is the sequence position of owner o's token i. Of the 16 positions held by one ctx shard (s * 16 to s * 16 + 15), at most 2 belong to one owner, and in every group some shard gives exactly 2 to some owner.
All inputs are finite; a program needn't handle non-finite values.
Results may differ from the reference program's by a relative error of at most 0.0057.
Values may be sent and summed in bfloat16 or wider, within the bound.
No kernel may reach another device: no remote copies, remote signals or barrier semaphores. Data moves between devices by JAX's collectives and lax.ppermute only.
A program may use at most 64 MiB of HBM per device.

```python
import math
import jax
import jax.numpy as jnp
from jax import lax

PATCH_W = 1280
MERGE = 4
D_IN = 5120
D_HID = 5120
D_OUT = 8192
M = 16
GROUP = 256
ROWS = 12288
N_DP = 48
N_CTX = 16
DEVICES = 768


def group_positions(group_key):
    share = M // N_CTX
    ranks = jnp.arange(N_CTX, dtype=jnp.int32)
    pattern = jnp.where(ranks < N_CTX // 4, 2 * share, jnp.where(ranks < 3 * N_CTX // 4, share, 0)).astype(jnp.int32)
    first_key, second_key, third_key = jax.random.split(group_key, 3)
    pattern = jax.random.permutation(first_key, pattern)
    shard_perm = jax.random.permutation(second_key, N_CTX).astype(jnp.int32)
    owner_perm = jax.random.permutation(third_key, N_CTX).astype(jnp.int32)
    counts = pattern[(shard_perm[:, None] - owner_perm[None, :]) % N_CTX]
    starts = ranks[:, None] * M + jnp.cumsum(counts, axis=1) - counts
    filled = jnp.cumsum(counts, axis=0)
    slot_ids = jnp.arange(M, dtype=jnp.int32)
    filled_owner = filled.T
    shard_of = jnp.sum((filled_owner[:, :, None] <= slot_ids[None, None, :]).astype(jnp.int32), axis=1)
    block_end = jnp.take_along_axis(filled_owner, shard_of, axis=1)
    block_count = jnp.take_along_axis(counts.T, shard_of, axis=1)
    block_start = jnp.take_along_axis(starts.T, shard_of, axis=1)
    position = block_start + slot_ids[None, :] - (block_end - block_count)
    return position.reshape(-1).astype(jnp.int32)


def draw_owner_pos(key, part):
    key = jax.random.fold_in(key, 11)
    group_keys = jax.random.split(key, N_DP)
    return jax.vmap(group_positions)(group_keys).reshape(-1)


def draw_grad_tokens(key, part):
    key = jax.random.fold_in(key, 5)
    fraction = jnp.arange(ROWS, dtype=jnp.float32) / ROWS
    values = jnp.clip(jax.random.normal(key, (ROWS, D_OUT), jnp.float32), -6.0, 6.0)
    row_scale = 0.5 + fraction
    return (values * row_scale[:, None]).astype(jnp.bfloat16)


def draw_patch_in(key, part):
    key = jax.random.fold_in(key, 7)
    base_key, row_key, col_key = jax.random.split(key, 3)
    total = ROWS * MERGE
    values = jnp.clip(jax.random.normal(base_key, (total, PATCH_W), jnp.float32), -6.0, 6.0)
    low_end = math.log(0.3)
    high_end = math.log(3.0)
    row_scale = jnp.exp(jax.random.uniform(row_key, (total, 1), jnp.float32, low_end, high_end))
    col_scale = jnp.exp(jax.random.uniform(col_key, (1, PATCH_W), jnp.float32, math.log(0.3), math.log(3.0)))
    return (values * row_scale * col_scale).reshape(ROWS, D_IN).astype(jnp.bfloat16)


def steps_of(stream_key, shape, shards, low, top_value):
    gain = 1.0
    for dim, blocks in shards:
        steps = jax.random.uniform(jax.random.fold_in(jax.random.fold_in(stream_key, 6), dim), (blocks,), jnp.float32, low / len(shards), top_value / len(shards))
        gain = gain * jnp.repeat(jnp.exp(steps), shape[dim] // blocks).reshape((-1,) + (1,) * (len(shape) - 1 - dim))
    return gain


def centred(own_key, extent, width, most, cuts=(), held_as=jnp.bfloat16):
    gain = steps_of(own_key, extent, cuts, -0.22, 0.18) if cuts else 1.0
    values = jax.random.normal(own_key, extent, jnp.float32) * width * gain
    return jnp.minimum(jnp.maximum(values, -most), most).astype(held_as)


def setup_inputs(seed: int = 0) -> dict:
    streams_of = jax.random.split(jax.random.key(seed), 8)
    return {
        "grad_tokens": draw_grad_tokens(jax.random.fold_in(streams_of[7], 71), 0),
        "pre_act": centred(streams_of[1], (D_HID, ROWS), 1.0, 6.0, ((0, 16), (1, 48))),
        "w_fc1": centred(streams_of[2], (D_IN, D_HID), D_IN ** -0.5, 0.078125, ((1, 16),)),
        "w_fc2": centred(streams_of[3], (D_HID, D_OUT), D_HID ** -0.5, 0.078125, ((1, 16),)),
        "patch_in": draw_patch_in(jax.random.fold_in(streams_of[7], 71), 0),
        "norm_gain": jnp.clip(1.0 + 0.15 * jax.random.normal(streams_of[5], (PATCH_W,), jnp.float32), 0.25, 1.75),
        "owner_pos": draw_owner_pos(jax.random.fold_in(streams_of[7], 71), 0),
    }


def gelu_slope(values):
    normal_cdf = 0.5 * (1.0 + lax.erf(values * 0.7071067811865476))
    density = jnp.exp(-0.5 * values * values) * 0.3989422804014327
    return normal_cdf + values * density

def reference(grad_tokens, pre_act, w_fc1, w_fc2, patch_in, norm_gain, owner_pos):
    token_grads = grad_tokens.reshape(N_DP, GROUP, D_OUT)
    saved_acts = pre_act.reshape(D_HID, N_DP, GROUP).transpose(1, 0, 2)
    positions = owner_pos.reshape(N_DP, GROUP)

    def one_group(inputs):
        group_grad, group_act, group_pos = inputs
        hidden_grad = jnp.dot(group_grad, w_fc2.T, preferred_element_type=jnp.float32)
        slope_values = gelu_slope(group_act.astype(jnp.float32)).T
        act_grad = (hidden_grad * slope_values).astype(jnp.bfloat16)
        merged_grad = jnp.dot(act_grad, w_fc1.T, preferred_element_type=jnp.float32).astype(jnp.bfloat16)
        return jnp.take(merged_grad, group_pos, axis=0)
    owner_grad = lax.map(one_group, (token_grads, saved_acts, positions)).reshape(ROWS, D_IN)
    upstream = owner_grad.astype(jnp.float32).reshape(ROWS * MERGE, PATCH_W)
    patches = patch_in.astype(jnp.float32).reshape(ROWS * MERGE, PATCH_W)
    inv_rms = lax.rsqrt(lax.optimization_barrier(jnp.mean(patches * patches, axis=-1, keepdims=True)) + 1e-06)
    normed = patches * inv_rms
    scaled_grad = upstream * norm_gain
    inner_mean = lax.optimization_barrier(jnp.mean(scaled_grad * normed, axis=-1, keepdims=True))
    patch_grad = (inv_rms * (scaled_grad - normed * inner_mean)).astype(jnp.bfloat16).reshape(ROWS, D_IN)
    gain_grad = lax.optimization_barrier(jnp.sum(upstream * normed, axis=0)) / DEVICES
    return (patch_grad, gain_grad)
```

```python
import functools

import jax
import jax.numpy as jnp
from jax import lax
from jax.experimental import pallas as pl
from jax.experimental.pallas import tpu as pltpu
from jax.sharding import Mesh
from jax.sharding import PartitionSpec as P

NY, NZL, NX, NZH, NCO = 8, 6, 4, 2, 2
AXES = ("y", "zl", "x", "zh", "co")
DP = ("y", "zl")
CTX = ("x", "zh", "co")
EPS = 1e-06
F32 = jnp.float32
BF16 = jnp.bfloat16
VMEM_LIMIT = 40 * 1024 * 1024


def gelu_slope(values):
    normal_cdf = 0.5 * (1.0 + lax.erf(values * 0.7071067811865476))
    density = jnp.exp(-0.5 * values * values) * 0.3989422804014327
    return normal_cdf + values * density


def params():
    return pltpu.CompilerParams(vmem_limit_bytes=VMEM_LIMIT)


def cost(flops, nbytes):
    return pl.CostEstimate(flops=flops, bytes_accessed=nbytes, transcendentals=0)


def swap(value, axis):
    return lax.ppermute(value, axis, [(0, 1), (1, 0)])


def hidden_kernel(which, w_ref, t_ref, out_ref):
    n, m = out_ref.shape[1], out_ref.shape[2]
    w = w_ref[...].reshape(n * m, w_ref.shape[-1])
    acc = lax.dot_general(w, t_ref[...], (((1,), (1,)), ((), ())), preferred_element_type=F32)
    out_ref[...] = acc.reshape(out_ref.shape).astype(out_ref.dtype)


def hidden_part(w_fc2, tokens, which, out_dtype):
    rows, depth = w_fc2.shape
    block = rows // (NX * NZH * NCO)
    count = tokens.shape[0]
    w = w_fc2.reshape(NX, NZH, NCO, block, depth)
    return pl.pallas_call(
        hidden_kernel,
        grid_spec=pltpu.PrefetchScalarGridSpec(
            num_scalar_prefetch=1,
            grid=(NX,),
            in_specs=[
                pl.BlockSpec((1, NZH, 1, block, depth), lambda i, s: (i, 0, s[0], 0, 0)),
                pl.BlockSpec((count, depth), lambda i, s: (0, 0)),
            ],
            out_specs=pl.BlockSpec((1, NZH, block, count), lambda i, s: (i, 0, 0, 0)),
        ),
        out_shape=jax.ShapeDtypeStruct((NX, NZH, block, count), out_dtype),
        compiler_params=params(),
        cost_estimate=cost(rows * depth * count, rows * depth + rows * count),
        name="hidden_part",
    )(which.reshape(1), w, tokens)


def add_kernel(a_ref, b_ref, out_ref):
    out_ref[...] = (a_ref[...] + b_ref[...].astype(F32)).astype(BF16)


def add_round(kept, got):
    shape = kept.shape
    blocks = shape[0]
    spec = pl.BlockSpec((1,) + shape[1:], lambda i: (i,) + (0,) * (len(shape) - 1))
    return pl.pallas_call(
        add_kernel,
        grid=(blocks,),
        in_specs=[spec, spec],
        out_specs=spec,
        out_shape=jax.ShapeDtypeStruct(shape, BF16),
        compiler_params=params(),
        cost_estimate=cost(kept.size, kept.size * 8),
        name="add_round",
    )(kept, got)


def sum_kernel(which, v_ref, out_ref):
    total = v_ref[0, 0].astype(F32)
    for i in range(1, v_ref.shape[0]):
        total += v_ref[i, 0].astype(F32)
    out_ref[...] = total.astype(BF16)


def sum_part(parts, which):
    n, two, rows, cols = parts.shape
    return pl.pallas_call(
        sum_kernel,
        grid_spec=pltpu.PrefetchScalarGridSpec(
            num_scalar_prefetch=1,
            grid=(1,),
            in_specs=[pl.BlockSpec((n, 1, rows, cols), lambda i, s: (0, s[0], 0, 0))],
            out_specs=pl.BlockSpec((rows, cols), lambda i, s: (0, 0)),
        ),
        out_shape=jax.ShapeDtypeStruct((rows, cols), BF16),
        compiler_params=params(),
        cost_estimate=cost(n * rows * cols, n * rows * cols * 2),
        name="sum_part",
    )(which.reshape(1), parts)


def act_kernel(which, v_ref, got_ref, slope_ref, pos_ref, out_ref):
    hidden = got_ref[...].astype(F32)
    for i in range(v_ref.shape[0]):
        hidden += v_ref[i, 0].astype(F32)
    act = (hidden * slope_ref[...]).astype(BF16)
    count = act.shape[1]
    pick = (pos_ref[...] == lax.broadcasted_iota(jnp.int32, (count, count), 1)).astype(F32).astype(BF16)
    out_ref[...] = lax.dot_general(pick, act, (((1,), (1,)), ((), ())), preferred_element_type=F32).astype(BF16)


def act_rows(parts, which, got, slope, positions):
    n, two, rows, cols = parts.shape
    return pl.pallas_call(
        act_kernel,
        grid_spec=pltpu.PrefetchScalarGridSpec(
            num_scalar_prefetch=1,
            grid=(1,),
            in_specs=[
                pl.BlockSpec((n, 1, rows, cols), lambda i, s: (0, s[0], 0, 0)),
                pl.BlockSpec((rows, cols), lambda i, s: (0, 0)),
                pl.BlockSpec((rows, cols), lambda i, s: (0, 0)),
                pl.BlockSpec((cols, 1), lambda i, s: (0, 0)),
            ],
            out_specs=pl.BlockSpec((cols, rows), lambda i, s: (0, 0)),
        ),
        out_shape=jax.ShapeDtypeStruct((cols, rows), BF16),
        compiler_params=params(),
        cost_estimate=cost(2 * rows * cols * cols, rows * cols * 16),
        name="act_rows",
    )(which.reshape(1), parts, got, slope, positions)


def merged_kernel(a_ref, w_ref, out_ref):
    acc = lax.dot_general(a_ref[...], w_ref[...], (((1,), (0,)), ((), ())), preferred_element_type=F32)
    out_ref[...] = acc.astype(out_ref.dtype)


def merged_part(act, w_fc1_t, out_dtype):
    rows, depth = act.shape
    cols = w_fc1_t.shape[1]
    steps = 4
    return pl.pallas_call(
        merged_kernel,
        grid=(steps,),
        in_specs=[
            pl.BlockSpec((rows, depth), lambda i: (0, 0)),
            pl.BlockSpec((depth, cols // steps), lambda i: (0, i)),
        ],
        out_specs=pl.BlockSpec((rows, cols // steps), lambda i: (0, i)),
        out_shape=jax.ShapeDtypeStruct((rows, cols), out_dtype),
        compiler_params=params(),
        cost_estimate=cost(2 * rows * depth * cols, depth * cols * 2),
        name="merged_part",
    )(act, w_fc1_t)


def norm_kernel(which, v_ref, got_ref, patch_ref, gain_ref, out_ref, terms_ref):
    width = gain_ref.shape[1]
    gain = gain_ref[...]
    terms = jnp.zeros((1, width), F32)
    for p in range(patch_ref.shape[1] // width):
        cols = pl.ds(p * width, width)
        owner = got_ref[:, cols].astype(F32)
        for i in range(v_ref.shape[0]):
            owner += v_ref[i, 0, :, cols].astype(F32)
        owner = owner.astype(BF16).astype(F32)
        patch = patch_ref[:, cols].astype(F32)
        inv_rms = lax.rsqrt(jnp.mean(patch * patch, axis=-1, keepdims=True) + EPS)
        normed = patch * inv_rms
        scaled = owner * gain
        inner = jnp.mean(scaled * normed, axis=-1, keepdims=True)
        out_ref[:, cols] = (inv_rms * (scaled - normed * inner)).astype(BF16)
        terms += jnp.sum(owner * normed, axis=0, keepdims=True)
    terms_ref[...] = terms


def norm_part(parts, which, got, patch_in, norm_gain):
    n, two, rows, cols = parts.shape
    width = norm_gain.shape[0]
    return pl.pallas_call(
        norm_kernel,
        grid_spec=pltpu.PrefetchScalarGridSpec(
            num_scalar_prefetch=1,
            grid=(1,),
            in_specs=[
                pl.BlockSpec((n, 1, rows, cols), lambda i, s: (0, s[0], 0, 0)),
                pl.BlockSpec((rows, cols), lambda i, s: (0, 0)),
                pl.BlockSpec((rows, cols), lambda i, s: (0, 0)),
                pl.BlockSpec((1, width), lambda i, s: (0, 0)),
            ],
            out_specs=[
                pl.BlockSpec((rows, cols), lambda i, s: (0, 0)),
                pl.BlockSpec((1, width), lambda i, s: (0, 0)),
            ],
        ),
        out_shape=[
            jax.ShapeDtypeStruct((rows, cols), BF16),
            jax.ShapeDtypeStruct((1, width), F32),
        ],
        compiler_params=params(),
        cost_estimate=cost(rows * cols * 20, rows * cols * 16),
        name="norm_part",
    )(which.reshape(1), parts, got, patch_in, norm_gain.reshape(1, width))


def local(grad_tokens, pre_act, w_fc1, w_fc2, patch_in, norm_gain, owner_pos):
    zh = lax.axis_index("zh").astype(jnp.int32)
    co = lax.axis_index("co").astype(jnp.int32)
    ctx = NX * NZH * NCO
    own, width = grad_tokens.shape
    group = own * ctx
    features = patch_in.shape[1]
    slope = gelu_slope(pre_act.astype(F32))
    by_core = owner_pos.reshape(NX * NZH, NCO, own)
    theirs = lax.dynamic_index_in_dim(by_core, 1 - co, axis=1, keepdims=False)
    mine = lax.dynamic_index_in_dim(by_core, co, axis=1, keepdims=False)
    positions = jnp.concatenate([theirs.reshape(-1, 1), mine.reshape(-1, 1)], axis=0)
    with jax.named_scope("tokens"):
        outgoing = grad_tokens.reshape(own, ctx, width // ctx).transpose(1, 0, 2)
        tokens = lax.all_to_all(outgoing, CTX, 0, 0, tiled=True).reshape(group, width // ctx)
    with jax.named_scope("hidden"):
        sent = hidden_part(w_fc2, tokens, 1 - co, BF16)
        got = swap(sent, "co")
        kept = hidden_part(w_fc2, tokens, co, F32)
        parts = add_round(kept, got)
        parts = lax.all_to_all(parts, "x", 0, 0, tiled=True)
        got = swap(sum_part(parts, 1 - zh), "zh")
    with jax.named_scope("merged"):
        act = act_rows(parts, zh, got, slope, positions)
        half = group // NCO
        w_fc1_t = w_fc1.T
        sent = merged_part(act[:half], w_fc1_t, BF16)
        got = swap(sent, "co")
        kept = merged_part(act[half:], w_fc1_t, F32)
        parts = add_round(
            kept.reshape(NX, NZH * own, features), got.reshape(NX, NZH * own, features)
        )
        parts = lax.all_to_all(parts, "x", 0, 0, tiled=True).reshape(NX, NZH, own, features)
        got = swap(sum_part(parts, 1 - zh), "zh")
    with jax.named_scope("norm"):
        patch_grad, terms = norm_part(parts, zh, got, patch_in, norm_gain)
    with jax.named_scope("gain"):
        terms = terms.reshape(-1)
        for axis in ("co", "x", "y"):
            terms = lax.psum(terms, axis)
        rows = terms.reshape(1, -1, 128)
        rows = jnp.broadcast_to(rows, (NZL * NZH,) + rows.shape[1:])
        rows = lax.all_to_all(rows, ("zl", "zh"), 0, 0, tiled=True)
        total = jnp.sum(rows, axis=0).reshape(-1)
        gain_grad = total / (NY * NZL * ctx)
    return (patch_grad, gain_grad)


def solution(mesh):
    fine = Mesh(mesh.devices.reshape(NY, NZL, NX, NZH, NCO), AXES)
    return jax.shard_map(
        local,
        mesh=fine,
        in_specs=(
            P(DP + CTX, None),
            P(CTX, DP),
            P(None, CTX),
            P(None, CTX),
            P(DP + CTX, None),
            P(),
            P(DP),
        ),
        out_specs=(P(DP + CTX, None), P()),
        check_vma=False,
    )
```

```python
import functools

import jax
import jax.numpy as jnp
from jax import lax
from jax.experimental import pallas as pl
from jax.experimental.pallas import tpu as pltpu
from jax.sharding import Mesh
from jax.sharding import PartitionSpec as P

NY, NZL, NX, NZH, NCO = 8, 6, 4, 2, 2
AXES = ("y", "zl", "x", "zh", "co")
DP = ("y", "zl")
CTX = ("x", "zh", "co")
EPS = 1e-06
F32 = jnp.float32
BF16 = jnp.bfloat16


def gelu_slope(values):
    normal_cdf = 0.5 * (1.0 + lax.erf(values * 0.7071067811865476))
    density = jnp.exp(-0.5 * values * values) * 0.3989422804014327
    return normal_cdf + values * density


def params(mib=12):
    return pltpu.CompilerParams(vmem_limit_bytes=mib * 1024 * 1024)


def cost():
    return pl.CostEstimate(flops=1, bytes_accessed=1, transcendentals=0)


def swap(value, axis):
    return lax.ppermute(value, axis, [(0, 1), (1, 0)])


def hidden_kernel(place, own_w, got_w, own_t, got_t, out_ref):
    total = None
    for w_ref, t_ref in ((own_w, own_t), (got_w, got_t)):
        term = lax.dot_general(
            w_ref[0, 0], t_ref[...], (((1,), (1,)), ((), ())), preferred_element_type=F32
        )
        total = term if total is None else total + term
    out_ref[0] = total.astype(BF16)


def hidden_part(weights, tokens, place):
    _, _, units, depth = weights[0].shape
    count = tokens[0].shape[0]
    w_spec = pl.BlockSpec((1, 1, units, depth), lambda i, s: (i, s[0], 0, 0))
    t_spec = pl.BlockSpec((count, depth), lambda i, s: (0, 0))
    return pl.pallas_call(
        hidden_kernel,
        grid_spec=pltpu.PrefetchScalarGridSpec(
            num_scalar_prefetch=1,
            grid=(NX,),
            in_specs=[w_spec, w_spec, t_spec, t_spec],
            out_specs=pl.BlockSpec((1, units, count), lambda i, s: (i, 0, 0)),
        ),
        out_shape=jax.ShapeDtypeStruct((NX, units, count), BF16),
        compiler_params=params(),
        cost_estimate=cost(),
        name="hidden_part",
    )(place, *weights, *tokens)


def total_of(ref):
    total = ref[0].astype(F32)
    for i in range(1, ref.shape[0]):
        total += ref[i].astype(F32)
    return total


def sum_kernel(v_ref, out_ref):
    out_ref[...] = total_of(v_ref).astype(BF16)


def sum_parts(parts):
    return pl.pallas_call(
        sum_kernel,
        out_shape=jax.ShapeDtypeStruct(parts.shape[1:], BF16),
        compiler_params=params(),
        cost_estimate=cost(),
        name="sum_parts",
    )(parts)


def act_kernel(v_ref, got_ref, slope_ref, pos_ref, out_ref):
    act = (total_of(v_ref) + got_ref[...].astype(F32)) * slope_ref[...]
    high = act.astype(BF16)
    low = (act - high.astype(F32)).astype(BF16)
    count = act.shape[1]
    pick = (lax.broadcasted_iota(jnp.int32, (count, count), 0) == pos_ref[...]).astype(F32)
    pick = pick.T.astype(BF16)
    for k, value in enumerate((high, low)):
        moved = lax.dot_general(pick, value, (((1,), (1,)), ((), ())), preferred_element_type=F32)
        out_ref[k] = moved.astype(BF16).reshape(out_ref.shape[1:])


def act_rows(parts, got, slope, owner_pos):
    units, count = got.shape
    return pl.pallas_call(
        act_kernel,
        out_shape=jax.ShapeDtypeStruct((2, NX, NZH, count // (NX * NZH), units), BF16),
        compiler_params=params(),
        cost_estimate=cost(),
        name="act_rows",
    )(parts, got, slope, owner_pos.reshape(1, count))


def merged_kernel(place, own_a, got_a, own_w, got_w, out_ref):
    depth = own_w.shape[0]
    total = None
    for a_ref, w_ref in ((own_a, own_w), (got_a, got_w)):
        term = lax.dot_general(
            a_ref[...].reshape(-1, depth),
            w_ref[...],
            (((1,), (0,)), ((), ())),
            preferred_element_type=F32,
        )
        total = term if total is None else total + term
    rows = total.shape[0] // 2
    out_ref[...] = (total[:rows] + total[rows:]).astype(BF16).reshape(out_ref.shape)


def merged_part(acts, weights, place):
    two, _, _, rows, depth = acts[0].shape
    cols = weights[0].shape[1]
    steps = 2
    a_spec = pl.BlockSpec((two, NX, 1, rows, depth), lambda i, s: (0, 0, s[0], 0, 0))
    w_spec = pl.BlockSpec((depth, cols // steps), lambda i, s: (0, i))
    return pl.pallas_call(
        merged_kernel,
        grid_spec=pltpu.PrefetchScalarGridSpec(
            num_scalar_prefetch=1,
            grid=(steps,),
            in_specs=[a_spec, a_spec, w_spec, w_spec],
            out_specs=pl.BlockSpec((NX, rows, cols // steps), lambda i, s: (0, 0, i)),
        ),
        out_shape=jax.ShapeDtypeStruct((NX, rows, cols), BF16),
        compiler_params=params(),
        cost_estimate=cost(),
        name="merged_part",
    )(place, *acts, *weights)


def halves_kernel(v_ref, out_ref):
    for c in range(NCO):
        total = v_ref[c].astype(F32)
        for x in range(1, NX):
            total += v_ref[NCO * x + c].astype(F32)
        out_ref[c] = total.astype(BF16)


def sum_halves(parts):
    return pl.pallas_call(
        halves_kernel,
        out_shape=jax.ShapeDtypeStruct((NCO,) + parts.shape[1:], BF16),
        compiler_params=params(),
        cost_estimate=cost(),
        name="sum_halves",
    )(parts)


def norm_of(patch):
    inv_rms = lax.rsqrt(jnp.mean(patch * patch, axis=-1, keepdims=True) + EPS)
    return patch * inv_rms, inv_rms


def gain_kernel(place, far_ref, near_ref, patch_ref, out_ref):
    width = out_ref.shape[1]
    terms = jnp.zeros((1, width), F32)
    for grad_ref, z in ((far_ref, 1 - place[0]), (near_ref, place[0])):
        for i in range(grad_ref.shape[0]):
            for p in range(grad_ref.shape[2] // width):
                cols = pl.ds(p * width, width)
                normed, _ = norm_of(patch_ref[i, z, :, cols].astype(F32))
                terms += jnp.sum(grad_ref[i, :, cols].astype(F32) * normed, axis=0, keepdims=True)
    out_ref[...] = terms


def gain_terms(far, near, patches, place, width):
    vmem = pl.BlockSpec(memory_space=pltpu.VMEM)
    return pl.pallas_call(
        gain_kernel,
        in_specs=[pl.BlockSpec(memory_space=pltpu.SMEM), vmem, vmem, vmem],
        out_specs=vmem,
        out_shape=jax.ShapeDtypeStruct((1, width), F32),
        compiler_params=params(),
        cost_estimate=cost(),
        name="gain_terms",
    )(place, far, near, patches)


def norm_kernel(v_ref, got_ref, patch_ref, gain_ref, out_ref):
    width = gain_ref.shape[1]
    gain = gain_ref[...]
    in_half = patch_ref.shape[1] // width // NCO
    for p in range(patch_ref.shape[1] // width):
        c, q = p // in_half, pl.ds(p % in_half * width, width)
        cols = pl.ds(p * width, width)
        owner = got_ref[c, :, q].astype(F32)
        for x in range(NX):
            owner += v_ref[NCO * x + c, :, q].astype(F32)
        normed, inv_rms = norm_of(patch_ref[:, cols].astype(F32))
        scaled = owner * gain
        inner = jnp.mean(scaled * normed, axis=-1, keepdims=True)
        out_ref[:, cols] = (inv_rms * (scaled - normed * inner)).astype(BF16)


def norm_part(parts, got, patch_in, norm_gain):
    return pl.pallas_call(
        norm_kernel,
        out_shape=jax.ShapeDtypeStruct(patch_in.shape, BF16),
        compiler_params=params(),
        cost_estimate=cost(),
        name="norm_part",
    )(parts, got, patch_in, norm_gain.reshape(1, -1))


def sum_over(terms, axes, count):
    rows = jnp.broadcast_to(terms[None], (count,) + terms.shape)
    return jnp.sum(lax.all_to_all(rows, axes, 0, 0, tiled=True), axis=0)


def local(grad_tokens, pre_act, w_fc1, w_fc2, patch_in, norm_gain, owner_pos):
    zh = lax.axis_index("zh").astype(jnp.int32)
    co = lax.axis_index("co").astype(jnp.int32)
    ctx = NX * NZH * NCO
    own, depth = grad_tokens.shape
    group = own * ctx
    width = norm_gain.shape[0]
    slope = gelu_slope(pre_act.astype(F32))
    far_z, near_z = (1 - zh).reshape(1), zh.reshape(1)
    features = patch_in.shape[1]
    half = features // NCO
    with jax.named_scope("tokens"):
        outgoing = grad_tokens.reshape(own, ctx, depth // ctx).transpose(1, 0, 2)
        outgoing, w_fc1, w_fc2, rows = lax.optimization_barrier((outgoing, w_fc1, w_fc2, patch_in))
        tokens = lax.all_to_all(outgoing, CTX, 0, 0, tiled=True).reshape(group, depth // ctx)
        tokens = (tokens, swap(tokens, "co"))
    with jax.named_scope("weights"):
        units = w_fc2.shape[0] // ctx
        w = w_fc2.reshape(NX, NZH, NCO, units, depth // ctx)
        take = lambda c: lax.dynamic_index_in_dim(w, c, axis=2, keepdims=False)
        weights_2 = (take(co), swap(take(1 - co), "co"))
        w_t = w_fc1.T
        take_1 = lambda c: lax.dynamic_slice_in_dim(w_t, c * half, half, axis=1)
        weights_1 = (take_1(co), swap(take_1(1 - co), "co"))
    with jax.named_scope("patches"):
        take_p = lambda c: lax.dynamic_slice_in_dim(rows, c * half, half, axis=1)
        kept, got = take_p(co), swap(take_p(1 - co), "co")
        both = jnp.where(co == 0, jnp.stack([kept, got]), jnp.stack([got, kept]))
        patches = lax.all_gather(both.reshape(NCO * own, half), ("x", "zh"))
        patches = patches.reshape(NX, NZH, NCO * own, half)
    with jax.named_scope("hidden"):
        far_sum = hidden_part(weights_2, tokens, far_z)
        far = lax.all_to_all(far_sum, "x", 0, 0, tiled=True)
        far = sum_parts(far)
        tokens, _ = lax.optimization_barrier((tokens, far))
        near_sum = hidden_part(weights_2, tokens, near_z)
        near = lax.all_to_all(near_sum, "x", 0, 0, tiled=True)
        got = swap(far, "zh")
    with jax.named_scope("merged"):
        act = act_rows(near, got, slope, owner_pos)
        acts = (act, swap(act, "co"))
        far_sum = merged_part(acts, weights_1, far_z)
        deliver = lambda v: lax.all_to_all(
            v.reshape(NX * NCO, own, half), ("x", "co"), 0, 0, tiled=True
        )
        far = deliver(far_sum)
        acts, _ = lax.optimization_barrier((acts, far_sum))
        near_sum = merged_part(acts, weights_1, near_z)
        far = sum_halves(far)
        late_sum, _ = lax.optimization_barrier((near_sum, far))
        near = deliver(late_sum)
        got = swap(far, "zh")
    with jax.named_scope("gain"):
        terms = gain_terms(far_sum, near_sum, patches, near_z, width).reshape(-1, 128)
        terms = lax.psum(lax.psum(terms, "co"), "x")
        terms, _ = lax.optimization_barrier((terms, near))
        terms = lax.psum(terms, "y")
        terms = sum_over(terms, ("zl", "zh"), NZL * NZH)
        gain_grad = terms.reshape(-1) / (NY * NZL * ctx)
    with jax.named_scope("norm"):
        patch_grad = norm_part(near, got, patch_in, norm_gain)
    return (patch_grad, gain_grad)


def solution(mesh):
    fine = Mesh(mesh.devices.reshape(NY, NZL, NX, NZH, NCO), AXES)
    return jax.shard_map(
        local,
        mesh=fine,
        in_specs=(
            P(DP + CTX, None),
            P(CTX, DP),
            P(None, CTX),
            P(None, CTX),
            P(DP + CTX, None),
            P(),
            P(DP),
        ),
        out_specs=(P(DP + CTX, None), P()),
        check_vma=False,
    )
```

```python
import functools

import jax
import jax.numpy as jnp
from jax import lax
from jax.experimental import pallas as pl
from jax.experimental.pallas import tpu as pltpu
from jax.sharding import Mesh
from jax.sharding import PartitionSpec as P

NY, NZL, NX, NZH, NCO = 8, 6, 4, 2, 2
AXES = ("y", "zl", "x", "zh", "co")
DP = ("y", "zl")
CTX = ("x", "zh", "co")
EPS = 1e-06
F32 = jnp.float32
BF16 = jnp.bfloat16


def gelu_slope(values):
    normal_cdf = 0.5 * (1.0 + lax.erf(values * 0.7071067811865476))
    density = jnp.exp(-0.5 * values * values) * 0.3989422804014327
    return normal_cdf + values * density


def params(mib=12):
    return pltpu.CompilerParams(vmem_limit_bytes=mib * 1024 * 1024)


def cost(flops=1):
    return pl.CostEstimate(flops=flops, bytes_accessed=1, transcendentals=0)


LONG = 20_000_000_000
ANYWHERE = pl.BlockSpec(memory_space=pl.ANY)
IN_VMEM = pl.BlockSpec(memory_space=pltpu.VMEM)
IN_SMEM = pl.BlockSpec(memory_space=pltpu.SMEM)


def swap(value, axis):
    return lax.ppermute(value, axis, [(0, 1), (1, 0)])


def hidden_kernel(place, own_w, got_w, own_t, got_t, out_ref, block, arrived):
    copies = [
        [
            pltpu.make_async_copy(w_ref.at[i, place[0], place[1]], block.at[i, k], arrived.at[i, k])
            for k, w_ref in enumerate((own_w, got_w))
        ]
        for i in range(NX)
    ]
    for pair in copies:
        for copy in pair:
            copy.start()
    for i, pair in enumerate(copies):
        total = None
        for k, t_ref in enumerate((own_t, got_t)):
            pair[k].wait()
            term = lax.dot_general(
                block[i, k], t_ref[...], (((1,), (1,)), ((), ())), preferred_element_type=F32
            )
            total = term if total is None else total + term
        out_ref[i] = total.astype(BF16)


def hidden_part(weights, tokens, place):
    rows, depth = weights[0].shape
    units = rows // (NX * NZH * NCO)
    count = tokens[0].shape[0]
    weights = [w.reshape(NX, NZH, NCO, units, depth) for w in weights]
    return pl.pallas_call(
        hidden_kernel,
        in_specs=[IN_SMEM, ANYWHERE, ANYWHERE, IN_VMEM, IN_VMEM],
        out_specs=IN_VMEM,
        out_shape=jax.ShapeDtypeStruct((NX, units, count), BF16),
        scratch_shapes=[
            pltpu.VMEM((NX, 2, units, depth), BF16),
            pltpu.SemaphoreType.DMA((NX, 2)),
        ],
        compiler_params=params(60),
        cost_estimate=cost(),
        name="hidden_part",
    )(place, *weights, *tokens)


def total_of(ref):
    total = ref[0].astype(F32)
    for i in range(1, ref.shape[0]):
        total += ref[i].astype(F32)
    return total


def sum_kernel(v_ref, out_ref):
    out_ref[...] = total_of(v_ref).astype(BF16)


def sum_parts(parts):
    return pl.pallas_call(
        sum_kernel,
        out_shape=jax.ShapeDtypeStruct(parts.shape[1:], BF16),
        compiler_params=params(),
        cost_estimate=cost(),
        name="sum_parts",
    )(parts)


def wide_kernel(v_ref, out_ref):
    out_ref[...] = v_ref[...].astype(F32)


def widen(value):
    return pl.pallas_call(
        wide_kernel,
        out_shape=jax.ShapeDtypeStruct(value.shape, F32),
        compiler_params=params(),
        cost_estimate=cost(LONG),
        name="widen",
    )(value)


def act_kernel(v_ref, got_ref, slope_ref, pos_ref, out_ref):
    act = ((total_of(v_ref) + got_ref[...]) * slope_ref[...]).astype(BF16)
    count = act.shape[1]
    pick = (lax.broadcasted_iota(jnp.int32, (count, count), 0) == pos_ref[...]).astype(F32)
    pick = pick.T.astype(BF16)
    moved = lax.dot_general(pick, act, (((1,), (1,)), ((), ())), preferred_element_type=F32)
    out_ref[...] = moved.astype(BF16).reshape(out_ref.shape)


def act_rows(parts, got, slope, owner_pos):
    units, count = got.shape
    return pl.pallas_call(
        act_kernel,
        out_shape=jax.ShapeDtypeStruct((NX, NZH, count // (NX * NZH), units), BF16),
        compiler_params=params(),
        cost_estimate=cost(),
        name="act_rows",
    )(parts, got, slope, owner_pos.reshape(1, count))


def merged_kernel(place, own_a, got_a, own_w, got_w, out_ref):
    depth = own_w.shape[0]
    total = None
    for a_ref, w_ref in ((own_a, own_w), (got_a, got_w)):
        term = lax.dot_general(
            a_ref[...].reshape(-1, depth),
            w_ref[...],
            (((1,), (0,)), ((), ())),
            preferred_element_type=F32,
        )
        total = term if total is None else total + term
    out_ref[...] = total.astype(BF16).reshape(out_ref.shape)


def merged_part(acts, weights, place):
    _, _, rows, depth = acts[0].shape
    cols = weights[0].shape[1] // NCO
    steps = 2
    a_spec = pl.BlockSpec((NX, 1, rows, depth), lambda i, s: (0, s[0], 0, 0))
    w_spec = pl.BlockSpec((depth, cols // steps), lambda i, s: (0, s[1] * steps + i))
    return pl.pallas_call(
        merged_kernel,
        grid_spec=pltpu.PrefetchScalarGridSpec(
            num_scalar_prefetch=1,
            grid=(steps,),
            in_specs=[a_spec, a_spec, w_spec, w_spec],
            out_specs=pl.BlockSpec((NX, rows, cols // steps), lambda i, s: (0, 0, i)),
        ),
        out_shape=jax.ShapeDtypeStruct((NX, rows, cols), BF16),
        compiler_params=params(),
        cost_estimate=cost(),
        name="merged_part",
    )(place, *acts, *weights)


def halves_kernel(v_ref, out_ref):
    for c in range(NCO):
        total = v_ref[c].astype(F32)
        for x in range(1, NX):
            total += v_ref[NCO * x + c].astype(F32)
        out_ref[c] = total.astype(BF16)


def sum_halves(parts):
    return pl.pallas_call(
        halves_kernel,
        out_shape=jax.ShapeDtypeStruct((NCO,) + parts.shape[1:], BF16),
        compiler_params=params(),
        cost_estimate=cost(),
        name="sum_halves",
    )(parts)


def norm_of(patch):
    inv_rms = lax.rsqrt(jnp.mean(patch * patch, axis=-1, keepdims=True) + EPS)
    return patch * inv_rms, inv_rms


def norm_kernel(v_ref, got_ref, patch_ref, gain_ref, out_ref, terms_ref):
    width = gain_ref.shape[1]
    gain = gain_ref[...]
    in_half = patch_ref.shape[1] // width // NCO
    terms = jnp.zeros((1, width), F32)
    for p in range(patch_ref.shape[1] // width):
        c, q = p // in_half, pl.ds(p % in_half * width, width)
        cols = pl.ds(p * width, width)
        owner = got_ref[c, :, q]
        for x in range(NX):
            owner += v_ref[NCO * x + c, :, q].astype(F32)
        normed, inv_rms = norm_of(patch_ref[:, cols].astype(F32))
        scaled = owner * gain
        inner = jnp.mean(scaled * normed, axis=-1, keepdims=True)
        out_ref[:, cols] = (inv_rms * (scaled - normed * inner)).astype(BF16)
        terms += jnp.sum(owner * normed, axis=0, keepdims=True)
    terms_ref[...] = terms


def norm_part(parts, got, patch_in, norm_gain):
    width = norm_gain.shape[0]
    return pl.pallas_call(
        norm_kernel,
        out_shape=[
            jax.ShapeDtypeStruct(patch_in.shape, BF16),
            jax.ShapeDtypeStruct((1, width), F32),
        ],
        compiler_params=params(),
        cost_estimate=cost(),
        name="norm_part",
    )(parts, got, patch_in, norm_gain.reshape(1, width))


def sum_over(terms, axes, count):
    rows = jnp.broadcast_to(terms[None], (count,) + terms.shape)
    return jnp.sum(lax.all_to_all(rows, axes, 0, 0, tiled=True), axis=0)


def local(grad_tokens, pre_act, w_fc1, w_fc2, patch_in, norm_gain, owner_pos):
    zh = lax.axis_index("zh").astype(jnp.int32)
    co = lax.axis_index("co").astype(jnp.int32)
    ctx = NX * NZH * NCO
    own, depth = grad_tokens.shape
    group = own * ctx
    slope = gelu_slope(pre_act.astype(F32))
    far_z, near_z = jnp.stack([1 - zh, co]), jnp.stack([zh, co])
    half = patch_in.shape[1] // NCO
    with jax.named_scope("tokens"):
        outgoing = grad_tokens.reshape(own, ctx, depth // ctx).transpose(1, 0, 2)
        tokens = lax.all_to_all(outgoing, CTX, 0, 0, tiled=True).reshape(group, depth // ctx)
        tokens = (tokens, swap(tokens, "co"))
    with jax.named_scope("weights"):
        weights_2 = (w_fc2, swap(w_fc2, "co"))
        w_fc1_t = w_fc1.T
        weights_1 = (w_fc1_t, swap(w_fc1_t, "co"))

    def exchange(part, deliver, add_up):
        far_sum = part(far_z, None)
        far = deliver(far_sum)
        near_sum = part(near_z, far_sum)
        far, near_sum = lax.optimization_barrier((far, near_sum))
        far = add_up(far)
        near_sum, _ = lax.optimization_barrier((near_sum, far))
        return deliver(near_sum), widen(swap(far, "zh"))

    def after(values, first):
        return values if first is None else lax.optimization_barrier((values, first))[0]

    with jax.named_scope("hidden"):
        near, got = exchange(
            lambda z, first: hidden_part(weights_2, after(tokens, first), z),
            lambda v: lax.all_to_all(v, "x", 0, 0, tiled=True),
            sum_parts,
        )
    with jax.named_scope("merged"):
        act = act_rows(near, got, slope, owner_pos)
        acts = (act, swap(act, "co"))
        near, got = exchange(
            lambda z, first: merged_part(after(acts, first), weights_1, z),
            lambda v: lax.all_to_all(
                v.reshape(NX * NCO, own, half), ("x", "co"), 0, 0, tiled=True
            ),
            sum_halves,
        )
    with jax.named_scope("norm"):
        patch_grad, terms = norm_part(near, got, patch_in, norm_gain)
    with jax.named_scope("gain"):
        terms = terms.reshape(-1, 128)
        terms = sum_over(terms, ("x", "co"), NX * NCO)
        terms = sum_over(terms, "y", NY)
        terms = sum_over(terms, ("zl", "zh"), NZL * NZH)
        gain_grad = terms.reshape(-1) / (NY * NZL * ctx)
    return (patch_grad, gain_grad)


def solution(mesh):
    fine = Mesh(mesh.devices.reshape(NY, NZL, NX, NZH, NCO), AXES)
    return jax.shard_map(
        local,
        mesh=fine,
        in_specs=(
            P(DP + CTX, None),
            P(CTX, DP),
            P(None, CTX),
            P(None, CTX),
            P(DP + CTX, None),
            P(),
            P(DP),
        ),
        out_specs=(P(DP + CTX, None), P()),
        check_vma=False,
    )
```

```python
import functools

import jax
import jax.numpy as jnp
from jax import lax
from jax.experimental import pallas as pl
from jax.experimental.pallas import tpu as pltpu
from jax.sharding import Mesh
from jax.sharding import PartitionSpec as P

NY, NZL, NX, NZH, NCO = 8, 6, 4, 2, 2
AXES = ("y", "zl", "x", "zh", "co")
DP = ("y", "zl")
CTX = ("x", "zh", "co")
EPS = 1e-06
F32 = jnp.float32
BF16 = jnp.bfloat16


def gelu_slope(values):
    normal_cdf = 0.5 * (1.0 + lax.erf(values * 0.7071067811865476))
    density = jnp.exp(-0.5 * values * values) * 0.3989422804014327
    return normal_cdf + values * density


def params(mib=12):
    return pltpu.CompilerParams(vmem_limit_bytes=mib * 1024 * 1024)


def cost(flops=1):
    return pl.CostEstimate(flops=flops, bytes_accessed=1, transcendentals=0)


LONG = 20_000_000_000
ANYWHERE = pl.BlockSpec(memory_space=pl.ANY)
IN_VMEM = pl.BlockSpec(memory_space=pltpu.VMEM)
IN_SMEM = pl.BlockSpec(memory_space=pltpu.SMEM)


def swap(value, axis):
    return lax.ppermute(value, axis, [(0, 1), (1, 0)])


def hidden_kernel(place, own_w, got_w, own_t, got_t, out_ref, block, tokens, arrived):
    depth = own_t.shape[1]
    copies = [
        [
            pltpu.make_async_copy(
                w_ref.at[i, place[0], place[1]],
                block.at[i, :, pl.ds(k * depth, depth)],
                arrived.at[i, k],
            )
            for k, w_ref in enumerate((own_w, got_w))
        ]
        for i in range(NX)
    ]
    for pair in copies:
        for copy in pair:
            copy.start()
    for k, t_ref in enumerate((own_t, got_t)):
        tokens[k * depth : (k + 1) * depth, :] = t_ref[...].T
    for i, pair in enumerate(copies):
        for copy in pair:
            copy.wait()
        total = lax.dot_general(
            block[i], tokens[...], (((1,), (0,)), ((), ())), preferred_element_type=F32
        )
        out_ref[i] = total.astype(BF16)


def hidden_part(weights, tokens, place):
    rows, depth = weights[0].shape
    units = rows // (NX * NZH * NCO)
    count = tokens[0].shape[0]
    weights = [w.reshape(NX, NZH, NCO, units, depth) for w in weights]
    return pl.pallas_call(
        hidden_kernel,
        in_specs=[IN_SMEM, ANYWHERE, ANYWHERE, IN_VMEM, IN_VMEM],
        out_specs=IN_VMEM,
        out_shape=jax.ShapeDtypeStruct((NX, units, count), BF16),
        scratch_shapes=[
            pltpu.VMEM((NX, units, 2 * depth), BF16),
            pltpu.VMEM((2 * depth, count), BF16),
            pltpu.SemaphoreType.DMA((NX, 2)),
        ],
        compiler_params=params(60),
        cost_estimate=cost(),
        name="hidden_part",
    )(place, *weights, *tokens)


def total_of(ref):
    total = ref[0].astype(F32)
    for i in range(1, ref.shape[0]):
        total += ref[i].astype(F32)
    return total


def sum_kernel(v_ref, out_ref):
    out_ref[...] = total_of(v_ref).astype(BF16)


def sum_parts(parts):
    return pl.pallas_call(
        sum_kernel,
        out_shape=jax.ShapeDtypeStruct(parts.shape[1:], BF16),
        compiler_params=params(),
        cost_estimate=cost(),
        name="sum_parts",
    )(parts)


def wide_kernel(v_ref, out_ref):
    out_ref[...] = v_ref[...].astype(F32)


def widen(value):
    return pl.pallas_call(
        wide_kernel,
        out_shape=jax.ShapeDtypeStruct(value.shape, F32),
        compiler_params=params(),
        cost_estimate=cost(LONG),
        name="widen",
    )(value)


def act_kernel(v_ref, got_ref, slope_ref, pos_ref, out_ref):
    act = ((total_of(v_ref) + got_ref[...]) * slope_ref[...]).astype(BF16)
    count = act.shape[1]
    pick = (lax.broadcasted_iota(jnp.int32, (count, count), 0) == pos_ref[...]).astype(F32)
    pick = pick.T.astype(BF16)
    moved = lax.dot_general(pick, act, (((1,), (1,)), ((), ())), preferred_element_type=F32)
    moved = moved.astype(BF16)
    own = out_ref.shape[3]
    for x in range(NX):
        for z in range(NZH):
            for c in range(NCO):
                first = ((x * NZH + z) * NCO + c) * own
                out_ref[x, c, z] = moved[first : first + own]


def act_rows(parts, got, slope, owner_pos):
    units, count = got.shape
    return pl.pallas_call(
        act_kernel,
        out_shape=jax.ShapeDtypeStruct((NX, NCO, NZH, count // (NX * NCO * NZH), units), BF16),
        compiler_params=params(),
        cost_estimate=cost(),
        name="act_rows",
    )(parts, got, slope, owner_pos.reshape(1, count))


def merged_kernel(place, own_a, got_a, own_w, got_w, out_ref):
    depth = own_w.shape[0]
    total = None
    for a_ref, w_ref in ((own_a, own_w), (got_a, got_w)):
        term = lax.dot_general(
            a_ref[...].reshape(-1, depth),
            w_ref[...],
            (((1,), (0,)), ((), ())),
            preferred_element_type=F32,
        )
        total = term if total is None else total + term
    out_ref[...] = total.astype(BF16).reshape(out_ref.shape)


def merged_part(acts, weights, core):
    depth = acts[0].shape[-1]
    cols = weights[0].shape[1] // NCO
    steps = 2
    a_spec = pl.BlockSpec(acts[0].shape, lambda i, s: (0, 0, 0, 0, 0))
    w_spec = pl.BlockSpec((depth, cols // steps), lambda i, s: (0, s[0] * steps + i))
    shape = acts[0].shape[:-1]
    return pl.pallas_call(
        merged_kernel,
        grid_spec=pltpu.PrefetchScalarGridSpec(
            num_scalar_prefetch=1,
            grid=(steps,),
            in_specs=[a_spec, a_spec, w_spec, w_spec],
            out_specs=pl.BlockSpec(shape + (cols // steps,), lambda i, s: (0, 0, 0, 0, i)),
        ),
        out_shape=jax.ShapeDtypeStruct(shape + (cols,), BF16),
        compiler_params=params(),
        cost_estimate=cost(),
        name="merged_part",
    )(core, *acts, *weights)


def halves_kernel(place, v_ref, out_ref):
    z = place[0]
    for c in range(NCO):
        total = v_ref[c, z].astype(F32)
        for x in range(1, NX):
            total += v_ref[NCO * x + c, z].astype(F32)
        out_ref[c] = total.astype(BF16)


def sum_halves(parts, place):
    return pl.pallas_call(
        halves_kernel,
        in_specs=[IN_SMEM, IN_VMEM],
        out_specs=IN_VMEM,
        out_shape=jax.ShapeDtypeStruct((NCO,) + parts.shape[2:], BF16),
        compiler_params=params(),
        cost_estimate=cost(),
        name="sum_halves",
    )(place, parts)


def pack_kernel(core, own_ref, got_ref, out_ref):
    half = out_ref.shape[2]
    cols = pl.ds(pl.multiple_of(core[0] * half, 128), half)
    out_ref[core[0]] = own_ref[:, cols]
    out_ref[1 - core[0]] = got_ref[:, cols]


def pack_patches(own, got, core):
    rows, cols = own.shape
    return pl.pallas_call(
        pack_kernel,
        in_specs=[IN_SMEM, IN_VMEM, IN_VMEM],
        out_specs=IN_VMEM,
        out_shape=jax.ShapeDtypeStruct((NCO, rows, cols // NCO), BF16),
        compiler_params=params(),
        cost_estimate=cost(),
        name="pack_patches",
    )(core, own, got)


def norm_of(patch):
    inv_rms = lax.rsqrt(jnp.mean(patch * patch, axis=-1, keepdims=True) + EPS)
    return patch * inv_rms, inv_rms


def gain_kernel(place, grad_ref, *refs):
    out_ref = refs[-1]
    width = out_ref.shape[1]
    terms = jnp.zeros((1, width), F32)
    for shift, patch_ref in enumerate(refs[:-1]):
        x = lax.rem(place[0] + shift, NX)
        for k in range(NZH):
            z = place[1] if k == 0 else 1 - place[1]
            for c in range(NCO):
                for p in range(grad_ref.shape[4] // width):
                    cols = pl.ds(p * width, width)
                    normed, _ = norm_of(patch_ref[k, c, :, cols].astype(F32))
                    grad = grad_ref[x, c, z, :, cols].astype(F32)
                    terms += jnp.sum(grad * normed, axis=0, keepdims=True)
    out_ref[...] = terms


def gain_terms(grads, patches, place, width):
    return pl.pallas_call(
        gain_kernel,
        in_specs=[IN_SMEM] + [IN_VMEM] * (1 + NX),
        out_specs=IN_VMEM,
        out_shape=jax.ShapeDtypeStruct((1, width), F32),
        compiler_params=params(),
        cost_estimate=cost(LONG),
        name="gain_terms",
    )(place, grads, *patches)


def norm_kernel(place, v_ref, got_ref, patch_ref, gain_ref, out_ref):
    width = gain_ref.shape[1]
    gain = gain_ref[...]
    z = place[0]
    in_half = patch_ref.shape[1] // width // NCO
    for p in range(patch_ref.shape[1] // width):
        c, q = p // in_half, pl.ds(p % in_half * width, width)
        cols = pl.ds(p * width, width)
        owner = got_ref[c, :, q].astype(F32)
        for x in range(NX):
            owner += v_ref[NCO * x + c, z, :, q].astype(F32)
        normed, inv_rms = norm_of(patch_ref[:, cols].astype(F32))
        scaled = owner * gain
        inner = jnp.mean(scaled * normed, axis=-1, keepdims=True)
        out_ref[:, cols] = (inv_rms * (scaled - normed * inner)).astype(BF16)


def norm_part(parts, got, patch_in, norm_gain, place):
    return pl.pallas_call(
        norm_kernel,
        in_specs=[IN_SMEM] + [IN_VMEM] * 4,
        out_specs=IN_VMEM,
        out_shape=jax.ShapeDtypeStruct(patch_in.shape, BF16),
        compiler_params=params(),
        cost_estimate=cost(LONG),
        name="norm_part",
    )(place, parts, got, patch_in, norm_gain.reshape(1, -1))


def sum_over(terms, axes, count):
    rows = jnp.broadcast_to(terms[None], (count,) + terms.shape)
    return jnp.sum(lax.all_to_all(rows, axes, 0, 0, tiled=True), axis=0)


def local(grad_tokens, pre_act, w_fc1, w_fc2, patch_in, norm_gain, owner_pos):
    zh = lax.axis_index("zh").astype(jnp.int32)
    co = lax.axis_index("co").astype(jnp.int32)
    ctx = NX * NZH * NCO
    own, depth = grad_tokens.shape
    group = own * ctx
    slope = gelu_slope(pre_act.astype(F32))
    far_z, near_z = jnp.stack([1 - zh, co]), jnp.stack([zh, co])
    half = patch_in.shape[1] // NCO
    with jax.named_scope("tokens"):
        outgoing = grad_tokens.reshape(own, ctx, depth // ctx).transpose(1, 0, 2)
        tokens = lax.all_to_all(outgoing, CTX, 0, 0, tiled=True).reshape(group, depth // ctx)
        tokens = (tokens, swap(tokens, "co"))
    with jax.named_scope("weights"):
        weights_2 = (w_fc2, swap(w_fc2, "co"))
        w_fc1_t = w_fc1.T
        weights_1 = (w_fc1_t, swap(w_fc1_t, "co"))

    with jax.named_scope("patches"):
        patches = pack_patches(patch_in, swap(patch_in, "co"), co.reshape(1))

    def tie(value, first):
        return lax.optimization_barrier((value, first))[0]

    with jax.named_scope("hidden"):
        far_sum = hidden_part(weights_2, tokens, far_z)
        far = lax.all_to_all(far_sum, "x", 0, 0, tiled=True)
        patches = jnp.stack([patches, swap(tie(patches, far_sum), "zh")])
        near_sum = hidden_part(weights_2, tie(tokens, far_sum), near_z)
        far, near_sum = lax.optimization_barrier((far, near_sum))
        far = sum_parts(far)
        near = lax.all_to_all(tie(near_sum, far), "x", 0, 0, tiled=True)
        got = widen(swap(far, "zh"))
        patches = tie(patches, far)
        around = [patches] + [
            lax.ppermute(patches, "x", [(i, (i - d) % NX) for i in range(NX)]) for d in (1, 2, 3)
        ]
    with jax.named_scope("merged"):
        act = act_rows(near, got, slope, owner_pos)
        grads = merged_part((act, swap(act, "co")), weights_1, co.reshape(1))
        parts = lax.all_to_all(
            grads.reshape(NX * NCO, NZH * own, half), ("x", "co"), 0, 0, tiled=True
        ).reshape(NX * NCO, NZH, own, half)
        here = jnp.stack([lax.axis_index("x").astype(jnp.int32), zh])
        terms = gain_terms(grads, around, here, norm_gain.shape[0]).reshape(-1, 128)
        terms = lax.psum(lax.psum(terms, "co"), "x")
        parts, terms = lax.optimization_barrier((parts, terms))
        far = sum_halves(parts, (1 - zh).reshape(1))
        got = swap(far, "zh")
    with jax.named_scope("gain"):
        terms = lax.psum(tie(terms, far), "y")
    with jax.named_scope("norm"):
        patch_grad = norm_part(parts, got, patch_in, norm_gain, zh.reshape(1))
    with jax.named_scope("gain"):
        terms = sum_over(terms, ("zl", "zh"), NZL * NZH)
        gain_grad = terms.reshape(-1) / (NY * NZL * ctx)
    return (patch_grad, gain_grad)


def solution(mesh):
    fine = Mesh(mesh.devices.reshape(NY, NZL, NX, NZH, NCO), AXES)
    return jax.shard_map(
        local,
        mesh=fine,
        in_specs=(
            P(DP + CTX, None),
            P(CTX, DP),
            P(None, CTX),
            P(None, CTX),
            P(DP + CTX, None),
            P(),
            P(DP),
        ),
        out_specs=(P(DP + CTX, None), P()),
        check_vma=False,
    )
```

```python
import functools

import jax
import jax.numpy as jnp
from jax import lax
from jax.experimental import pallas as pl
from jax.experimental.pallas import tpu as pltpu
from jax.sharding import Mesh
from jax.sharding import PartitionSpec as P

NY, NZL, NX, NZH, NCO = 8, 6, 4, 2, 2
AXES = ("y", "zl", "x", "zh", "co")
DP = ("y", "zl")
CTX = ("x", "zh", "co")
EPS = 1e-06
F32 = jnp.float32
BF16 = jnp.bfloat16


def gelu_slope(values):
    normal_cdf = 0.5 * (1.0 + lax.erf(values * 0.7071067811865476))
    density = jnp.exp(-0.5 * values * values) * 0.3989422804014327
    return normal_cdf + values * density


def params(mib=12):
    return pltpu.CompilerParams(vmem_limit_bytes=mib * 1024 * 1024)


def cost(flops=1):
    return pl.CostEstimate(flops=flops, bytes_accessed=1, transcendentals=0)


LONG = 20_000_000_000
ANYWHERE = pl.BlockSpec(memory_space=pl.ANY)
IN_VMEM = pl.BlockSpec(memory_space=pltpu.VMEM)
IN_SMEM = pl.BlockSpec(memory_space=pltpu.SMEM)


def swap(value, axis):
    return lax.ppermute(value, axis, [(0, 1), (1, 0)])


def hidden_kernel(core, own_w, got_w, own_t, got_t, out_ref):
    depth = own_t.shape[1]
    total = None
    for w_ref, t_ref in ((own_w, own_t), (got_w, got_t)):
        term = lax.dot_general(
            w_ref[...].reshape(-1, depth),
            t_ref[...],
            (((1,), (1,)), ((), ())),
            preferred_element_type=F32,
        )
        total = term if total is None else total + term
    out_ref[...] = total.astype(BF16).reshape(out_ref.shape)


def hidden_part(weights, tokens, core):
    rows, depth = weights[0].shape
    units = rows // (NX * NZH * NCO)
    count = tokens[0].shape[0]
    weights = [w.reshape(NX, NZH, NCO, units, depth) for w in weights]
    w_spec = pl.BlockSpec((1, NZH, 1, units, depth), lambda i, s: (i, 0, s[0], 0, 0))
    t_spec = pl.BlockSpec((count, depth), lambda i, s: (0, 0))
    return pl.pallas_call(
        hidden_kernel,
        grid_spec=pltpu.PrefetchScalarGridSpec(
            num_scalar_prefetch=1,
            grid=(NX,),
            in_specs=[w_spec, w_spec, t_spec, t_spec],
            out_specs=pl.BlockSpec((1, NZH, units, count), lambda i, s: (i, 0, 0, 0)),
        ),
        out_shape=jax.ShapeDtypeStruct((NX, NZH, units, count), BF16),
        compiler_params=params(60),
        cost_estimate=cost(),
        name="hidden_part",
    )(core, *weights, *tokens)


def total_of(ref, z):
    total = ref[0, z].astype(F32)
    for i in range(1, ref.shape[0]):
        total += ref[i, z].astype(F32)
    return total


def sum_kernel(place, v_ref, out_ref):
    out_ref[...] = total_of(v_ref, place[0]).astype(BF16)


def sum_parts(parts, place):
    return pl.pallas_call(
        sum_kernel,
        in_specs=[IN_SMEM, IN_VMEM],
        out_specs=IN_VMEM,
        out_shape=jax.ShapeDtypeStruct(parts.shape[2:], BF16),
        compiler_params=params(),
        cost_estimate=cost(),
        name="sum_parts",
    )(place, parts)


def act_kernel(place, v_ref, got_ref, slope_ref, pos_ref, out_ref):
    act = ((total_of(v_ref, place[0]) + got_ref[...].astype(F32)) * slope_ref[...]).astype(BF16)
    count = act.shape[1]
    pick = (lax.broadcasted_iota(jnp.int32, (count, count), 0) == pos_ref[...]).astype(F32)
    pick = pick.T.astype(BF16)
    moved = lax.dot_general(pick, act, (((1,), (1,)), ((), ())), preferred_element_type=F32)
    moved = moved.astype(BF16)
    own = out_ref.shape[3]
    for x in range(NX):
        for z in range(NZH):
            for c in range(NCO):
                first = ((x * NZH + z) * NCO + c) * own
                out_ref[x, c, z] = moved[first : first + own]


def act_rows(parts, got, slope, owner_pos, place):
    units, count = got.shape
    return pl.pallas_call(
        act_kernel,
        in_specs=[IN_SMEM] + [IN_VMEM] * 4,
        out_specs=IN_VMEM,
        out_shape=jax.ShapeDtypeStruct((NX, NCO, NZH, count // (NX * NCO * NZH), units), BF16),
        compiler_params=params(),
        cost_estimate=cost(),
        name="act_rows",
    )(place, parts, got, slope, owner_pos.reshape(1, count))


def merged_kernel(place, own_a, got_a, own_w, got_w, out_ref):
    depth = own_w.shape[0]
    total = None
    for a_ref, w_ref in ((own_a, own_w), (got_a, got_w)):
        term = lax.dot_general(
            a_ref[...].reshape(-1, depth),
            w_ref[...],
            (((1,), (0,)), ((), ())),
            preferred_element_type=F32,
        )
        total = term if total is None else total + term
    out_ref[...] = total.astype(BF16).reshape(out_ref.shape)


def merged_part(acts, weights, core):
    depth = acts[0].shape[-1]
    cols = weights[0].shape[1] // NCO
    steps = 2
    a_spec = pl.BlockSpec(acts[0].shape, lambda i, s: (0, 0, 0, 0, 0))
    w_spec = pl.BlockSpec((depth, cols // steps), lambda i, s: (0, s[0] * steps + i))
    shape = acts[0].shape[:-1]
    return pl.pallas_call(
        merged_kernel,
        grid_spec=pltpu.PrefetchScalarGridSpec(
            num_scalar_prefetch=1,
            grid=(steps,),
            in_specs=[a_spec, a_spec, w_spec, w_spec],
            out_specs=pl.BlockSpec(shape + (cols // steps,), lambda i, s: (0, 0, 0, 0, i)),
        ),
        out_shape=jax.ShapeDtypeStruct(shape + (cols,), BF16),
        compiler_params=params(),
        cost_estimate=cost(),
        name="merged_part",
    )(core, *acts, *weights)


def halves_kernel(place, v_ref, out_ref):
    z = place[0]
    for c in range(NCO):
        total = v_ref[c, z].astype(F32)
        for x in range(1, NX):
            total += v_ref[NCO * x + c, z].astype(F32)
        out_ref[c] = total.astype(BF16)


def sum_halves(parts, place):
    return pl.pallas_call(
        halves_kernel,
        in_specs=[IN_SMEM, IN_VMEM],
        out_specs=IN_VMEM,
        out_shape=jax.ShapeDtypeStruct((NCO,) + parts.shape[2:], BF16),
        compiler_params=params(),
        cost_estimate=cost(),
        name="sum_halves",
    )(place, parts)


def pack_kernel(core, own_ref, got_ref, out_ref):
    half = out_ref.shape[2]
    cols = pl.ds(pl.multiple_of(core[0] * half, 128), half)
    out_ref[core[0]] = own_ref[:, cols]
    out_ref[1 - core[0]] = got_ref[:, cols]


def pack_patches(own, got, core):
    rows, cols = own.shape
    return pl.pallas_call(
        pack_kernel,
        in_specs=[IN_SMEM, IN_VMEM, IN_VMEM],
        out_specs=IN_VMEM,
        out_shape=jax.ShapeDtypeStruct((NCO, rows, cols // NCO), BF16),
        compiler_params=params(),
        cost_estimate=cost(),
        name="pack_patches",
    )(core, own, got)


def norm_of(patch):
    inv_rms = lax.rsqrt(jnp.mean(patch * patch, axis=-1, keepdims=True) + EPS)
    return patch * inv_rms, inv_rms


def gain_kernel(place, grad_ref, *refs):
    out_ref = refs[-1]
    width = out_ref.shape[1]
    terms = jnp.zeros((1, width), F32)
    for shift, patch_ref in enumerate(refs[:-1]):
        x = lax.rem(place[0] + shift, NX)
        for k in range(NZH):
            z = place[1] if k == 0 else 1 - place[1]
            for c in range(NCO):
                for p in range(grad_ref.shape[4] // width):
                    cols = pl.ds(p * width, width)
                    normed, _ = norm_of(patch_ref[k, c, :, cols].astype(F32))
                    grad = grad_ref[x, c, z, :, cols].astype(F32)
                    terms += jnp.sum(grad * normed, axis=0, keepdims=True)
    out_ref[...] = terms


def gain_terms(grads, patches, place, width):
    return pl.pallas_call(
        gain_kernel,
        in_specs=[IN_SMEM] + [IN_VMEM] * (1 + NX),
        out_specs=IN_VMEM,
        out_shape=jax.ShapeDtypeStruct((1, width), F32),
        compiler_params=params(),
        cost_estimate=cost(LONG),
        name="gain_terms",
    )(place, grads, *patches)


def norm_kernel(place, v_ref, got_ref, patch_ref, gain_ref, out_ref):
    width = gain_ref.shape[1]
    gain = gain_ref[...]
    z = place[0]
    in_half = patch_ref.shape[1] // width // NCO
    for p in range(patch_ref.shape[1] // width):
        c, q = p // in_half, pl.ds(p % in_half * width, width)
        cols = pl.ds(p * width, width)
        owner = got_ref[c, :, q].astype(F32)
        for x in range(NX):
            owner += v_ref[NCO * x + c, z, :, q].astype(F32)
        normed, inv_rms = norm_of(patch_ref[:, cols].astype(F32))
        scaled = owner * gain
        inner = jnp.mean(scaled * normed, axis=-1, keepdims=True)
        out_ref[:, cols] = (inv_rms * (scaled - normed * inner)).astype(BF16)


def norm_part(parts, got, patch_in, norm_gain, place):
    return pl.pallas_call(
        norm_kernel,
        in_specs=[IN_SMEM] + [IN_VMEM] * 4,
        out_specs=IN_VMEM,
        out_shape=jax.ShapeDtypeStruct(patch_in.shape, BF16),
        compiler_params=params(),
        cost_estimate=cost(LONG),
        name="norm_part",
    )(place, parts, got, patch_in, norm_gain.reshape(1, -1))


def sum_over(terms, axes, count):
    rows = jnp.broadcast_to(terms[None], (count,) + terms.shape)
    return jnp.sum(lax.all_to_all(rows, axes, 0, 0, tiled=True), axis=0)


def local(grad_tokens, pre_act, w_fc1, w_fc2, patch_in, norm_gain, owner_pos):
    zh = lax.axis_index("zh").astype(jnp.int32)
    co = lax.axis_index("co").astype(jnp.int32)
    ctx = NX * NZH * NCO
    own, depth = grad_tokens.shape
    group = own * ctx
    slope = gelu_slope(pre_act.astype(F32))
    far_z, near_z, core = (1 - zh).reshape(1), zh.reshape(1), co.reshape(1)
    half = patch_in.shape[1] // NCO
    with jax.named_scope("tokens"):
        outgoing = grad_tokens.reshape(own, ctx, depth // ctx).transpose(1, 0, 2)
        tokens = lax.all_to_all(outgoing, CTX, 0, 0, tiled=True).reshape(group, depth // ctx)
        tokens = (tokens, swap(tokens, "co"))
    with jax.named_scope("weights"):
        weights_2 = (w_fc2, swap(w_fc2, "co"))
        w_fc1_t = w_fc1.T

    with jax.named_scope("patches"):
        patches = pack_patches(patch_in, swap(patch_in, "co"), core)

    def tie(value, first):
        return lax.optimization_barrier((value, first))[0]

    with jax.named_scope("hidden"):
        sums = hidden_part(weights_2, tokens, core)
        parts = lax.all_to_all(sums, "x", 0, 0, tiled=True)
        ready = tie(patches, sums)
        weights_1 = (w_fc1_t, swap(tie(w_fc1_t, ready), "co"))
        beyond = swap(ready, "zh")
        far = sum_parts(parts, far_z)
        got = swap(far, "zh")
        patches = jnp.stack([tie(patches, far), beyond])
        around = [patches] + [
            lax.ppermute(patches, "x", [(i, (i - d) % NX) for i in range(NX)]) for d in (1, 2, 3)
        ]
    with jax.named_scope("merged"):
        act = act_rows(parts, got, slope, owner_pos, near_z)
        sums = merged_part((act, swap(act, "co")), weights_1, core)
        parts = lax.all_to_all(
            sums.reshape(NX * NCO, NZH * own, half), ("x", "co"), 0, 0, tiled=True
        ).reshape(NX * NCO, NZH, own, half)
        here = jnp.stack([lax.axis_index("x").astype(jnp.int32), zh])
        terms = gain_terms(sums, around, here, norm_gain.shape[0]).reshape(-1, 128)
        terms = lax.psum(lax.psum(terms, "co"), "y")
        parts, terms = lax.optimization_barrier((parts, terms))
        far = sum_halves(parts, far_z)
        got = swap(far, "zh")
    with jax.named_scope("gain"):
        terms = lax.psum(tie(terms, far), "x")
    with jax.named_scope("norm"):
        patch_grad = norm_part(parts, got, patch_in, norm_gain, near_z)
    with jax.named_scope("gain"):
        terms = sum_over(terms, ("zl", "zh"), NZL * NZH)
        gain_grad = terms.reshape(-1) / (NY * NZL * ctx)
    return (patch_grad, gain_grad)


def solution(mesh):
    fine = Mesh(mesh.devices.reshape(NY, NZL, NX, NZH, NCO), AXES)
    return jax.shard_map(
        local,
        mesh=fine,
        in_specs=(
            P(DP + CTX, None),
            P(CTX, DP),
            P(None, CTX),
            P(None, CTX),
            P(DP + CTX, None),
            P(),
            P(DP),
        ),
        out_specs=(P(DP + CTX, None), P()),
        check_vma=False,
    )
```

```python
import functools

import jax
import jax.numpy as jnp
from jax import lax
from jax.experimental import pallas as pl
from jax.experimental.pallas import tpu as pltpu
from jax.sharding import Mesh
from jax.sharding import PartitionSpec as P

NY, NZL, NX, NZH, NCO = 8, 6, 4, 2, 2
AXES = ("y", "zl", "x", "zh", "co")
DP = ("y", "zl")
CTX = ("x", "zh", "co")
EPS = 1e-06
F32 = jnp.float32
BF16 = jnp.bfloat16


def gelu_slope(values):
    normal_cdf = 0.5 * (1.0 + lax.erf(values * 0.7071067811865476))
    density = jnp.exp(-0.5 * values * values) * 0.3989422804014327
    return normal_cdf + values * density


def params(mib=12):
    return pltpu.CompilerParams(vmem_limit_bytes=mib * 1024 * 1024)


def cost(flops=1):
    return pl.CostEstimate(flops=flops, bytes_accessed=1, transcendentals=0)


LONG = 20_000_000_000
ANYWHERE = pl.BlockSpec(memory_space=pl.ANY)
IN_VMEM = pl.BlockSpec(memory_space=pltpu.VMEM)
IN_SMEM = pl.BlockSpec(memory_space=pltpu.SMEM)


def swap(value, axis):
    return lax.ppermute(value, axis, [(0, 1), (1, 0)])


def hidden_kernel(core, own_w, got_w, own_t, got_t, out_ref):
    depth = own_t.shape[1]
    total = None
    for w_ref, t_ref in ((own_w, own_t), (got_w, got_t)):
        term = lax.dot_general(
            w_ref[...].reshape(-1, depth),
            t_ref[...],
            (((1,), (1,)), ((), ())),
            preferred_element_type=F32,
        )
        total = term if total is None else total + term
    out_ref[...] = total.astype(BF16).reshape(out_ref.shape)


def hidden_part(weights, tokens, core):
    rows, depth = weights[0].shape
    units = rows // (NX * NZH * NCO)
    count = tokens[0].shape[0]
    weights = [w.reshape(NX, NZH, NCO, units, depth) for w in weights]
    w_spec = pl.BlockSpec((1, NZH, 1, units, depth), lambda i, s: (i, 0, s[0], 0, 0))
    t_spec = pl.BlockSpec((count, depth), lambda i, s: (0, 0))
    return pl.pallas_call(
        hidden_kernel,
        grid_spec=pltpu.PrefetchScalarGridSpec(
            num_scalar_prefetch=1,
            grid=(NX,),
            in_specs=[w_spec, w_spec, t_spec, t_spec],
            out_specs=pl.BlockSpec((1, NZH, units, count), lambda i, s: (i, 0, 0, 0)),
        ),
        out_shape=jax.ShapeDtypeStruct((NX, NZH, units, count), BF16),
        compiler_params=params(60),
        cost_estimate=cost(),
        name="hidden_part",
    )(core, *weights, *tokens)


def total_of(ref, z):
    total = ref[0, z].astype(F32)
    for i in range(1, ref.shape[0]):
        total += ref[i, z].astype(F32)
    return total


def sum_kernel(place, v_ref, out_ref):
    out_ref[...] = total_of(v_ref, place[0]).astype(BF16)


def sum_parts(parts, place):
    return pl.pallas_call(
        sum_kernel,
        in_specs=[IN_SMEM, IN_VMEM],
        out_specs=IN_VMEM,
        out_shape=jax.ShapeDtypeStruct(parts.shape[2:], BF16),
        compiler_params=params(),
        cost_estimate=cost(),
        name="sum_parts",
    )(place, parts)


def act_kernel(place, v_ref, got_ref, slope_ref, pos_ref, out_ref):
    act = ((total_of(v_ref, place[0]) + got_ref[...].astype(F32)) * slope_ref[...]).astype(BF16)
    count = act.shape[1]
    pick = (lax.broadcasted_iota(jnp.int32, (count, count), 0) == pos_ref[...]).astype(F32)
    pick = pick.T.astype(BF16)
    moved = lax.dot_general(pick, act, (((1,), (1,)), ((), ())), preferred_element_type=F32)
    moved = moved.astype(BF16)
    own = out_ref.shape[3]
    for x in range(NX):
        for z in range(NZH):
            for c in range(NCO):
                first = ((x * NZH + z) * NCO + c) * own
                out_ref[x, c, z] = moved[first : first + own]


def act_rows(parts, got, slope, owner_pos, place):
    units, count = got.shape
    return pl.pallas_call(
        act_kernel,
        in_specs=[IN_SMEM] + [IN_VMEM] * 4,
        out_specs=IN_VMEM,
        out_shape=jax.ShapeDtypeStruct((NX, NCO, NZH, count // (NX * NCO * NZH), units), BF16),
        compiler_params=params(),
        cost_estimate=cost(),
        name="act_rows",
    )(place, parts, got, slope, owner_pos.reshape(1, count))


def merged_kernel(place, own_a, got_a, own_w, got_w, out_ref):
    depth = own_w.shape[0]
    total = None
    for a_ref, w_ref in ((own_a, own_w), (got_a, got_w)):
        term = lax.dot_general(
            a_ref[...].reshape(-1, depth),
            w_ref[...],
            (((1,), (0,)), ((), ())),
            preferred_element_type=F32,
        )
        total = term if total is None else total + term
    out_ref[...] = total.astype(BF16).reshape(out_ref.shape)


def merged_part(acts, weights, core):
    depth = acts[0].shape[-1]
    cols = weights[0].shape[1] // NCO
    steps = 2
    a_spec = pl.BlockSpec(acts[0].shape, lambda i, s: (0, 0, 0, 0, 0))
    w_spec = pl.BlockSpec((depth, cols // steps), lambda i, s: (0, s[0] * steps + i))
    shape = acts[0].shape[:-1]
    return pl.pallas_call(
        merged_kernel,
        grid_spec=pltpu.PrefetchScalarGridSpec(
            num_scalar_prefetch=1,
            grid=(steps,),
            in_specs=[a_spec, a_spec, w_spec, w_spec],
            out_specs=pl.BlockSpec(shape + (cols // steps,), lambda i, s: (0, 0, 0, 0, i)),
        ),
        out_shape=jax.ShapeDtypeStruct(shape + (cols,), BF16),
        compiler_params=params(),
        cost_estimate=cost(),
        name="merged_part",
    )(core, *acts, *weights)


def halves_kernel(place, v_ref, out_ref):
    z = place[0]
    for c in range(NCO):
        total = v_ref[c, z].astype(F32)
        for x in range(1, NX):
            total += v_ref[NCO * x + c, z].astype(F32)
        out_ref[c] = total.astype(BF16)


def sum_halves(parts, place):
    return pl.pallas_call(
        halves_kernel,
        in_specs=[IN_SMEM, IN_VMEM],
        out_specs=IN_VMEM,
        out_shape=jax.ShapeDtypeStruct((NCO,) + parts.shape[2:], BF16),
        compiler_params=params(),
        cost_estimate=cost(),
        name="sum_halves",
    )(place, parts)


def pack_kernel(core, own_ref, got_ref, out_ref):
    half = out_ref.shape[2]
    cols = pl.ds(pl.multiple_of(core[0] * half, 128), half)
    out_ref[core[0]] = own_ref[:, cols]
    out_ref[1 - core[0]] = got_ref[:, cols]


def pack_patches(own, got, core):
    rows, cols = own.shape
    return pl.pallas_call(
        pack_kernel,
        in_specs=[IN_SMEM, IN_VMEM, IN_VMEM],
        out_specs=IN_VMEM,
        out_shape=jax.ShapeDtypeStruct((NCO, rows, cols // NCO), BF16),
        compiler_params=params(),
        cost_estimate=cost(),
        name="pack_patches",
    )(core, own, got)


def norm_of(patch):
    inv_rms = lax.rsqrt(jnp.mean(patch * patch, axis=-1, keepdims=True) + EPS)
    return patch * inv_rms, inv_rms


def gain_kernel(place, grad_ref, *refs):
    out_ref = refs[-1]
    width = out_ref.shape[1]
    terms = jnp.zeros((1, width), F32)
    for shift, patch_ref in enumerate(refs[:-1]):
        x = lax.rem(place[0] + shift, NX)
        for k in range(NZH):
            z = place[1] if k == 0 else 1 - place[1]
            for c in range(NCO):
                for p in range(grad_ref.shape[4] // width):
                    cols = pl.ds(p * width, width)
                    normed, _ = norm_of(patch_ref[k, c, :, cols].astype(F32))
                    grad = grad_ref[x, c, z, :, cols].astype(F32)
                    terms += jnp.sum(grad * normed, axis=0, keepdims=True)
    out_ref[...] = terms


def gain_terms(grads, patches, place, width):
    return pl.pallas_call(
        gain_kernel,
        in_specs=[IN_SMEM] + [IN_VMEM] * (1 + NX),
        out_specs=IN_VMEM,
        out_shape=jax.ShapeDtypeStruct((1, width), F32),
        compiler_params=params(),
        cost_estimate=cost(LONG),
        name="gain_terms",
    )(place, grads, *patches)


def norm_kernel(place, v_ref, got_ref, patch_ref, gain_ref, out_ref):
    width = gain_ref.shape[1]
    gain = gain_ref[...]
    z = place[0]
    in_half = patch_ref.shape[1] // width // NCO
    for p in range(patch_ref.shape[1] // width):
        c, q = p // in_half, pl.ds(p % in_half * width, width)
        cols = pl.ds(p * width, width)
        owner = got_ref[c, :, q].astype(F32)
        for x in range(NX):
            owner += v_ref[NCO * x + c, z, :, q].astype(F32)
        normed, inv_rms = norm_of(patch_ref[:, cols].astype(F32))
        scaled = owner * gain
        inner = jnp.mean(scaled * normed, axis=-1, keepdims=True)
        out_ref[:, cols] = (inv_rms * (scaled - normed * inner)).astype(BF16)


def norm_part(parts, got, patch_in, norm_gain, place):
    return pl.pallas_call(
        norm_kernel,
        in_specs=[IN_SMEM] + [IN_VMEM] * 4,
        out_specs=IN_VMEM,
        out_shape=jax.ShapeDtypeStruct(patch_in.shape, BF16),
        compiler_params=params(),
        cost_estimate=cost(LONG),
        name="norm_part",
    )(place, parts, got, patch_in, norm_gain.reshape(1, -1))


def sum_over(terms, axes, count):
    rows = jnp.broadcast_to(terms[None], (count,) + terms.shape)
    return jnp.sum(lax.all_to_all(rows, axes, 0, 0, tiled=True), axis=0)


def local(grad_tokens, pre_act, w_fc1, w_fc2, patch_in, norm_gain, owner_pos):
    zh = lax.axis_index("zh").astype(jnp.int32)
    co = lax.axis_index("co").astype(jnp.int32)
    ctx = NX * NZH * NCO
    own, depth = grad_tokens.shape
    group = own * ctx
    slope = gelu_slope(pre_act.astype(F32))
    far_z, near_z, core = (1 - zh).reshape(1), zh.reshape(1), co.reshape(1)
    half = patch_in.shape[1] // NCO
    with jax.named_scope("tokens"):
        outgoing = grad_tokens.reshape(own, ctx, depth // ctx).transpose(1, 0, 2)
        tokens = lax.all_to_all(outgoing, CTX, 0, 0, tiled=True).reshape(group, depth // ctx)
        beside = swap(patch_in, "co")
        tokens, beside = lax.optimization_barrier((tokens, beside))
        tokens = (tokens, swap(tokens, "co"))
    with jax.named_scope("weights"):
        weights_2 = (w_fc2, swap(w_fc2, "co"))
        w_fc1_t = w_fc1.T

    with jax.named_scope("patches"):
        patches = pack_patches(patch_in, beside, core)

    def tie(value, first):
        return lax.optimization_barrier((value, first))[0]

    with jax.named_scope("hidden"):
        sums = hidden_part(weights_2, tokens, core)
        parts = lax.all_to_all(sums, "x", 0, 0, tiled=True)
        ready = tie(patches, sums)
        weights_1 = (w_fc1_t, swap(tie(w_fc1_t, ready), "co"))
        beyond = swap(ready, "zh")
        far = sum_parts(parts, far_z)
        got = swap(far, "zh")
        patches = jnp.stack([tie(patches, far), beyond])
        around = [patches] + [
            lax.ppermute(patches, "x", [(i, (i - d) % NX) for i in range(NX)]) for d in (1, 2, 3)
        ]
    with jax.named_scope("merged"):
        act = act_rows(parts, got, slope, owner_pos, near_z)
        sums = merged_part((act, swap(act, "co")), weights_1, core)
        parts = lax.all_to_all(
            sums.reshape(NX * NCO, NZH * own, half), ("x", "co"), 0, 0, tiled=True
        ).reshape(NX * NCO, NZH, own, half)
        here = jnp.stack([lax.axis_index("x").astype(jnp.int32), zh])
        terms = gain_terms(sums, around, here, norm_gain.shape[0]).reshape(-1, 128)
        terms = lax.psum(terms, "co")
        parts, terms = lax.optimization_barrier((parts, terms))
        far = sum_halves(parts, far_z)
        got = swap(far, "zh")
    with jax.named_scope("gain"):
        terms = sum_over(tie(terms, far), ("x", "y"), NX * NY)
    with jax.named_scope("norm"):
        patch_grad = norm_part(parts, got, patch_in, norm_gain, near_z)
    with jax.named_scope("gain"):
        terms = sum_over(terms, ("zl", "zh"), NZL * NZH)
        gain_grad = terms.reshape(-1) / (NY * NZL * ctx)
    return (patch_grad, gain_grad)


def solution(mesh):
    fine = Mesh(mesh.devices.reshape(NY, NZL, NX, NZH, NCO), AXES)
    return jax.shard_map(
        local,
        mesh=fine,
        in_specs=(
            P(DP + CTX, None),
            P(CTX, DP),
            P(None, CTX),
            P(None, CTX),
            P(DP + CTX, None),
            P(),
            P(DP),
        ),
        out_specs=(P(DP + CTX, None), P()),
        check_vma=False,
    )
```

```python
import functools

import jax
import jax.numpy as jnp
from jax import lax
from jax.experimental import pallas as pl
from jax.experimental.pallas import tpu as pltpu
from jax.sharding import Mesh
from jax.sharding import PartitionSpec as P

NY, NZL, NX, NZH, NCO = 8, 6, 4, 2, 2
AXES = ("y", "zl", "x", "zh", "co")
DP = ("y", "zl")
CTX = ("x", "zh", "co")
EPS = 1e-06
F32 = jnp.float32
BF16 = jnp.bfloat16


def gelu_slope(values):
    normal_cdf = 0.5 * (1.0 + lax.erf(values * 0.7071067811865476))
    density = jnp.exp(-0.5 * values * values) * 0.3989422804014327
    return normal_cdf + values * density


def params(mib=12):
    return pltpu.CompilerParams(vmem_limit_bytes=mib * 1024 * 1024)


def cost(flops=1):
    return pl.CostEstimate(flops=flops, bytes_accessed=1, transcendentals=0)


LONG = 20_000_000_000
ANYWHERE = pl.BlockSpec(memory_space=pl.ANY)
IN_VMEM = pl.BlockSpec(memory_space=pltpu.VMEM)
IN_SMEM = pl.BlockSpec(memory_space=pltpu.SMEM)


def swap(value, axis):
    return lax.ppermute(value, axis, [(0, 1), (1, 0)])


def hidden_kernel(core, own_w, got_w, own_t, got_t, out_ref):
    depth = own_t.shape[1]
    total = None
    for w_ref, t_ref in ((own_w, own_t), (got_w, got_t)):
        term = lax.dot_general(
            w_ref[...].reshape(-1, depth),
            t_ref[...],
            (((1,), (1,)), ((), ())),
            preferred_element_type=F32,
        )
        total = term if total is None else total + term
    out_ref[...] = total.astype(BF16).reshape(out_ref.shape)


def hidden_part(weights, tokens, core):
    rows, depth = weights[0].shape
    units = rows // (NX * NZH * NCO)
    count = tokens[0].shape[0]
    weights = [w.reshape(NX, NZH, NCO, units, depth) for w in weights]
    w_spec = pl.BlockSpec((1, NZH, 1, units, depth), lambda i, s: (i, 0, s[0], 0, 0))
    t_spec = pl.BlockSpec((count, depth), lambda i, s: (0, 0))
    return pl.pallas_call(
        hidden_kernel,
        grid_spec=pltpu.PrefetchScalarGridSpec(
            num_scalar_prefetch=1,
            grid=(NX,),
            in_specs=[w_spec, w_spec, t_spec, t_spec],
            out_specs=pl.BlockSpec((1, NZH, units, count), lambda i, s: (i, 0, 0, 0)),
        ),
        out_shape=jax.ShapeDtypeStruct((NX, NZH, units, count), BF16),
        compiler_params=params(60),
        cost_estimate=cost(),
        name="hidden_part",
    )(core, *weights, *tokens)


def total_of(ref, z):
    total = ref[0, z].astype(F32)
    for i in range(1, ref.shape[0]):
        total += ref[i, z].astype(F32)
    return total


def sum_kernel(place, v_ref, out_ref):
    out_ref[...] = total_of(v_ref, place[0]).astype(BF16)


def sum_parts(parts, place):
    return pl.pallas_call(
        sum_kernel,
        in_specs=[IN_SMEM, IN_VMEM],
        out_specs=IN_VMEM,
        out_shape=jax.ShapeDtypeStruct(parts.shape[2:], BF16),
        compiler_params=params(),
        cost_estimate=cost(),
        name="sum_parts",
    )(place, parts)


def wide_kernel(v_ref, out_ref):
    out_ref[...] = v_ref[...].astype(F32)


def widen(value):
    return pl.pallas_call(
        wide_kernel,
        out_shape=jax.ShapeDtypeStruct(value.shape, F32),
        compiler_params=params(),
        cost_estimate=cost(LONG),
        name="widen",
    )(value)


def act_kernel(place, v_ref, got_ref, slope_ref, pos_ref, out_ref):
    act = ((total_of(v_ref, place[0]) + got_ref[...]) * slope_ref[...]).astype(BF16)
    count = act.shape[1]
    pick = (lax.broadcasted_iota(jnp.int32, (count, count), 0) == pos_ref[...]).astype(F32)
    pick = pick.T.astype(BF16)
    moved = lax.dot_general(pick, act, (((1,), (1,)), ((), ())), preferred_element_type=F32)
    moved = moved.astype(BF16)
    own = out_ref.shape[3]
    for x in range(NX):
        for z in range(NZH):
            for c in range(NCO):
                first = ((x * NZH + z) * NCO + c) * own
                out_ref[x, c, z] = moved[first : first + own]


def act_rows(parts, got, slope, owner_pos, place):
    units, count = got.shape
    return pl.pallas_call(
        act_kernel,
        in_specs=[IN_SMEM] + [IN_VMEM] * 4,
        out_specs=IN_VMEM,
        out_shape=jax.ShapeDtypeStruct((NX, NCO, NZH, count // (NX * NCO * NZH), units), BF16),
        compiler_params=params(),
        cost_estimate=cost(),
        name="act_rows",
    )(place, parts, got, slope, owner_pos.reshape(1, count))


def merged_kernel(place, own_a, got_a, own_w, got_w, out_ref):
    depth = own_w.shape[0]
    total = None
    for a_ref, w_ref in ((own_a, own_w), (got_a, got_w)):
        term = lax.dot_general(
            a_ref[...].reshape(-1, depth),
            w_ref[...],
            (((1,), (0,)), ((), ())),
            preferred_element_type=F32,
        )
        total = term if total is None else total + term
    out_ref[...] = total.astype(BF16).reshape(out_ref.shape)


def merged_part(acts, weights, core):
    depth = acts[0].shape[-1]
    cols = weights[0].shape[1] // NCO
    steps = 2
    a_spec = pl.BlockSpec(acts[0].shape, lambda i, s: (0, 0, 0, 0, 0))
    w_spec = pl.BlockSpec((depth, cols // steps), lambda i, s: (0, s[0] * steps + i))
    shape = acts[0].shape[:-1]
    return pl.pallas_call(
        merged_kernel,
        grid_spec=pltpu.PrefetchScalarGridSpec(
            num_scalar_prefetch=1,
            grid=(steps,),
            in_specs=[a_spec, a_spec, w_spec, w_spec],
            out_specs=pl.BlockSpec(shape + (cols // steps,), lambda i, s: (0, 0, 0, 0, i)),
        ),
        out_shape=jax.ShapeDtypeStruct(shape + (cols,), BF16),
        compiler_params=params(),
        cost_estimate=cost(),
        name="merged_part",
    )(core, *acts, *weights)


def halves_kernel(place, v_ref, out_ref):
    z = place[0]
    for c in range(NCO):
        total = v_ref[c, z].astype(F32)
        for x in range(1, NX):
            total += v_ref[NCO * x + c, z].astype(F32)
        out_ref[c] = total.astype(BF16)


def sum_halves(parts, place):
    return pl.pallas_call(
        halves_kernel,
        in_specs=[IN_SMEM, IN_VMEM],
        out_specs=IN_VMEM,
        out_shape=jax.ShapeDtypeStruct((NCO,) + parts.shape[2:], BF16),
        compiler_params=params(),
        cost_estimate=cost(),
        name="sum_halves",
    )(place, parts)


def pack_kernel(core, own_ref, got_ref, out_ref):
    half = out_ref.shape[2]
    cols = pl.ds(pl.multiple_of(core[0] * half, 128), half)
    out_ref[core[0]] = own_ref[:, cols]
    out_ref[1 - core[0]] = got_ref[:, cols]


def pack_patches(own, got, core):
    rows, cols = own.shape
    return pl.pallas_call(
        pack_kernel,
        in_specs=[IN_SMEM, IN_VMEM, IN_VMEM],
        out_specs=IN_VMEM,
        out_shape=jax.ShapeDtypeStruct((NCO, rows, cols // NCO), BF16),
        compiler_params=params(),
        cost_estimate=cost(),
        name="pack_patches",
    )(core, own, got)


def spread_kernel(own_ref, beyond_ref, out_ref):
    for x in range(NX):
        out_ref[x, 0] = own_ref[...]
        out_ref[x, 1] = beyond_ref[...]


def spread_patches(own, beyond):
    return pl.pallas_call(
        spread_kernel,
        out_shape=jax.ShapeDtypeStruct((NX, NZH) + own.shape, BF16),
        compiler_params=params(),
        cost_estimate=cost(),
        name="spread_patches",
    )(own, beyond)


def norm_of(patch):
    inv_rms = lax.rsqrt(jnp.mean(patch * patch, axis=-1, keepdims=True) + EPS)
    return patch * inv_rms, inv_rms


def gain_kernel(place, grad_ref, patch_ref, out_ref):
    width = out_ref.shape[1]
    terms = jnp.zeros((1, width), F32)
    for x in range(NX):
        for k in range(NZH):
            z = place[0] if k == 0 else 1 - place[0]
            for c in range(NCO):
                for p in range(grad_ref.shape[4] // width):
                    cols = pl.ds(p * width, width)
                    normed, _ = norm_of(patch_ref[x, k, c, :, cols].astype(F32))
                    grad = grad_ref[x, c, z, :, cols].astype(F32)
                    terms += jnp.sum(grad * normed, axis=0, keepdims=True)
    out_ref[...] = terms


def gain_terms(grads, patches, place, width):
    return pl.pallas_call(
        gain_kernel,
        in_specs=[IN_SMEM] + [IN_VMEM] * 2,
        out_specs=IN_VMEM,
        out_shape=jax.ShapeDtypeStruct((1, width), F32),
        compiler_params=params(),
        cost_estimate=cost(LONG),
        name="gain_terms",
    )(place, grads, patches)


def norm_kernel(place, v_ref, got_ref, patch_ref, gain_ref, out_ref):
    width = gain_ref.shape[1]
    gain = gain_ref[...]
    z = place[0]
    in_half = patch_ref.shape[1] // width // NCO
    for p in range(patch_ref.shape[1] // width):
        c, q = p // in_half, pl.ds(p % in_half * width, width)
        cols = pl.ds(p * width, width)
        owner = got_ref[c, :, q].astype(F32)
        for x in range(NX):
            owner += v_ref[NCO * x + c, z, :, q].astype(F32)
        normed, inv_rms = norm_of(patch_ref[:, cols].astype(F32))
        scaled = owner * gain
        inner = jnp.mean(scaled * normed, axis=-1, keepdims=True)
        out_ref[:, cols] = (inv_rms * (scaled - normed * inner)).astype(BF16)


def norm_part(parts, got, patch_in, norm_gain, place):
    return pl.pallas_call(
        norm_kernel,
        in_specs=[IN_SMEM] + [IN_VMEM] * 4,
        out_specs=IN_VMEM,
        out_shape=jax.ShapeDtypeStruct(patch_in.shape, BF16),
        compiler_params=params(),
        cost_estimate=cost(LONG),
        name="norm_part",
    )(place, parts, got, patch_in, norm_gain.reshape(1, -1))


def sum_over(terms, axes, count):
    rows = jnp.broadcast_to(terms[None], (count,) + terms.shape)
    return jnp.sum(lax.all_to_all(rows, axes, 0, 0, tiled=True), axis=0)


def local(grad_tokens, pre_act, w_fc1, w_fc2, patch_in, norm_gain, owner_pos):
    zh = lax.axis_index("zh").astype(jnp.int32)
    co = lax.axis_index("co").astype(jnp.int32)
    ctx = NX * NZH * NCO
    own, depth = grad_tokens.shape
    group = own * ctx
    slope = gelu_slope(pre_act.astype(F32))
    far_z, near_z, core = (1 - zh).reshape(1), zh.reshape(1), co.reshape(1)
    half = patch_in.shape[1] // NCO
    with jax.named_scope("tokens"):
        outgoing = grad_tokens.reshape(own, ctx, depth // ctx).transpose(1, 0, 2)
        tokens = lax.all_to_all(outgoing, CTX, 0, 0, tiled=True).reshape(group, depth // ctx)
        beside = swap(patch_in, "co")
        tokens, beside = lax.optimization_barrier((tokens, beside))
        tokens = (tokens, swap(tokens, "co"))
    with jax.named_scope("weights"):
        weights_2 = (w_fc2, swap(w_fc2, "co"))
        w_fc1_t = w_fc1.T

    with jax.named_scope("patches"):
        patches = pack_patches(patch_in, beside, core)

    def tie(value, first):
        return lax.optimization_barrier((value, first))[0]

    with jax.named_scope("hidden"):
        sums = hidden_part(weights_2, tokens, core)
        parts = lax.all_to_all(sums, "x", 0, 0, tiled=True)
        ready = tie(patches, sums)
        weights_1 = (w_fc1_t, swap(tie(w_fc1_t, ready), "co"))
        beyond = swap(ready, "zh")
        far = sum_parts(parts, far_z)
        got = widen(swap(far, "zh"))
        around = spread_patches(tie(patches, far), beyond)
        around = lax.all_to_all(around, "x", 0, 0, tiled=True)
    with jax.named_scope("merged"):
        act = act_rows(parts, got, slope, owner_pos, near_z)
        sums = merged_part((act, swap(act, "co")), weights_1, core)
        parts = lax.all_to_all(
            sums.reshape(NX * NCO, NZH * own, half), ("x", "co"), 0, 0, tiled=True
        ).reshape(NX * NCO, NZH, own, half)
        terms = gain_terms(sums, around, near_z, norm_gain.shape[0]).reshape(-1, 128)
        terms = lax.psum(terms, "y")
        parts, terms = lax.optimization_barrier((parts, terms))
        far = sum_halves(parts, far_z)
        got = swap(far, "zh")
    with jax.named_scope("gain"):
        terms = sum_over(tie(terms, far), ("x", "co"), NX * NCO)
    with jax.named_scope("norm"):
        patch_grad = norm_part(parts, got, patch_in, norm_gain, near_z)
    with jax.named_scope("gain"):
        terms = sum_over(terms, ("zl", "zh"), NZL * NZH)
        gain_grad = terms.reshape(-1) / (NY * NZL * ctx)
    return (patch_grad, gain_grad)


def solution(mesh):
    fine = Mesh(mesh.devices.reshape(NY, NZL, NX, NZH, NCO), AXES)
    return jax.shard_map(
        local,
        mesh=fine,
        in_specs=(
            P(DP + CTX, None),
            P(CTX, DP),
            P(None, CTX),
            P(None, CTX),
            P(DP + CTX, None),
            P(),
            P(DP),
        ),
        out_specs=(P(DP + CTX, None), P()),
        check_vma=False,
    )
```

```python
import functools

import jax
import jax.numpy as jnp
from jax import lax
from jax.experimental import pallas as pl
from jax.experimental.pallas import tpu as pltpu
from jax.sharding import Mesh
from jax.sharding import PartitionSpec as P

NY, NZL, NX, NZH, NCO = 8, 6, 4, 2, 2
AXES = ("y", "zl", "x", "zh", "co")
DP = ("y", "zl")
CTX = ("x", "zh", "co")
EPS = 1e-06
F32 = jnp.float32
BF16 = jnp.bfloat16


def gelu_slope(values):
    normal_cdf = 0.5 * (1.0 + lax.erf(values * 0.7071067811865476))
    density = jnp.exp(-0.5 * values * values) * 0.3989422804014327
    return normal_cdf + values * density


def params(mib=12):
    return pltpu.CompilerParams(vmem_limit_bytes=mib * 1024 * 1024)


def cost(flops=1):
    return pl.CostEstimate(flops=flops, bytes_accessed=1, transcendentals=0)


LONG = 20_000_000_000
ANYWHERE = pl.BlockSpec(memory_space=pl.ANY)
IN_VMEM = pl.BlockSpec(memory_space=pltpu.VMEM)
IN_SMEM = pl.BlockSpec(memory_space=pltpu.SMEM)


def swap(value, axis):
    return lax.ppermute(value, axis, [(0, 1), (1, 0)])


def hidden_kernel(core, own_w, got_w, own_t, got_t, out_ref):
    depth = own_t.shape[1]
    total = None
    for w_ref, t_ref in ((own_w, own_t), (got_w, got_t)):
        term = lax.dot_general(
            w_ref[...].reshape(-1, depth),
            t_ref[...],
            (((1,), (1,)), ((), ())),
            preferred_element_type=F32,
        )
        total = term if total is None else total + term
    out_ref[...] = total.astype(BF16).reshape(out_ref.shape)


def hidden_part(weights, tokens, core):
    rows, depth = weights[0].shape
    units = rows // (NX * NZH * NCO)
    count = tokens[0].shape[0]
    weights = [w.reshape(NX, NZH, NCO, units, depth) for w in weights]
    w_spec = pl.BlockSpec((1, NZH, 1, units, depth), lambda i, s: (i, 0, s[0], 0, 0))
    t_spec = pl.BlockSpec((count, depth), lambda i, s: (0, 0))
    return pl.pallas_call(
        hidden_kernel,
        grid_spec=pltpu.PrefetchScalarGridSpec(
            num_scalar_prefetch=1,
            grid=(NX,),
            in_specs=[w_spec, w_spec, t_spec, t_spec],
            out_specs=pl.BlockSpec((1, NZH, units, count), lambda i, s: (i, 0, 0, 0)),
        ),
        out_shape=jax.ShapeDtypeStruct((NX, NZH, units, count), BF16),
        compiler_params=params(52),
        cost_estimate=cost(),
        name="hidden_part",
    )(core, *weights, *tokens)


def total_of(ref, z):
    total = ref[0, z].astype(F32)
    for i in range(1, ref.shape[0]):
        total += ref[i, z].astype(F32)
    return total


def sum_kernel(place, v_ref, out_ref):
    out_ref[...] = total_of(v_ref, place[0]).astype(BF16)


def sum_parts(parts, place):
    return pl.pallas_call(
        sum_kernel,
        in_specs=[IN_SMEM, IN_VMEM],
        out_specs=IN_VMEM,
        out_shape=jax.ShapeDtypeStruct(parts.shape[2:], BF16),
        compiler_params=params(),
        cost_estimate=cost(),
        name="sum_parts",
    )(place, parts)


def wide_kernel(v_ref, out_ref):
    out_ref[...] = v_ref[...].astype(F32)


def widen(value):
    return pl.pallas_call(
        wide_kernel,
        out_shape=jax.ShapeDtypeStruct(value.shape, F32),
        compiler_params=params(),
        cost_estimate=cost(LONG),
        name="widen",
    )(value)


def act_kernel(place, v_ref, got_ref, slope_ref, pos_ref, out_ref):
    act = ((total_of(v_ref, place[0]) + got_ref[...]) * slope_ref[...]).astype(BF16)
    count = act.shape[1]
    pick = (lax.broadcasted_iota(jnp.int32, (count, count), 0) == pos_ref[...]).astype(F32)
    pick = pick.T.astype(BF16)
    moved = lax.dot_general(pick, act, (((1,), (1,)), ((), ())), preferred_element_type=F32)
    moved = moved.astype(BF16)
    own = out_ref.shape[3]
    for x in range(NX):
        for z in range(NZH):
            for c in range(NCO):
                first = ((x * NZH + z) * NCO + c) * own
                out_ref[x, c, z] = moved[first : first + own]


def act_rows(parts, got, slope, owner_pos, place):
    units, count = got.shape
    return pl.pallas_call(
        act_kernel,
        in_specs=[IN_SMEM] + [IN_VMEM] * 4,
        out_specs=IN_VMEM,
        out_shape=jax.ShapeDtypeStruct((NX, NCO, NZH, count // (NX * NCO * NZH), units), BF16),
        compiler_params=params(),
        cost_estimate=cost(),
        name="act_rows",
    )(place, parts, got, slope, owner_pos.reshape(1, count))


def merged_kernel(place, own_a, got_a, own_w, got_w, out_ref):
    depth = own_w.shape[0]
    total = None
    for a_ref, w_ref in ((own_a, own_w), (got_a, got_w)):
        term = lax.dot_general(
            a_ref[...].reshape(-1, depth),
            w_ref[...],
            (((1,), (0,)), ((), ())),
            preferred_element_type=F32,
        )
        total = term if total is None else total + term
    out_ref[...] = total.astype(BF16).reshape(out_ref.shape)


def merged_part(acts, weights, core):
    depth = acts[0].shape[-1]
    cols = weights[0].shape[1] // NCO
    steps = 2
    a_spec = pl.BlockSpec(acts[0].shape, lambda i, s: (0, 0, 0, 0, 0))
    w_spec = pl.BlockSpec((depth, cols // steps), lambda i, s: (0, s[0] * steps + i))
    shape = acts[0].shape[:-1]
    return pl.pallas_call(
        merged_kernel,
        grid_spec=pltpu.PrefetchScalarGridSpec(
            num_scalar_prefetch=1,
            grid=(steps,),
            in_specs=[a_spec, a_spec, w_spec, w_spec],
            out_specs=pl.BlockSpec(shape + (cols // steps,), lambda i, s: (0, 0, 0, 0, i)),
        ),
        out_shape=jax.ShapeDtypeStruct(shape + (cols,), BF16),
        compiler_params=params(),
        cost_estimate=cost(),
        name="merged_part",
    )(core, *acts, *weights)


def halves_kernel(place, v_ref, out_ref):
    z = place[0]
    for c in range(NCO):
        total = v_ref[c, z].astype(F32)
        for x in range(1, NX):
            total += v_ref[NCO * x + c, z].astype(F32)
        out_ref[c] = total.astype(BF16)


def sum_halves(parts, place):
    return pl.pallas_call(
        halves_kernel,
        in_specs=[IN_SMEM, IN_VMEM],
        out_specs=IN_VMEM,
        out_shape=jax.ShapeDtypeStruct((NCO,) + parts.shape[2:], BF16),
        compiler_params=params(),
        cost_estimate=cost(),
        name="sum_halves",
    )(place, parts)


def pack_kernel(core, own_ref, got_ref, out_ref):
    half = out_ref.shape[2]
    cols = pl.ds(pl.multiple_of(core[0] * half, 128), half)
    out_ref[core[0]] = own_ref[:, cols]
    out_ref[1 - core[0]] = got_ref[:, cols]


def pack_patches(own, got, core):
    rows, cols = own.shape
    return pl.pallas_call(
        pack_kernel,
        in_specs=[IN_SMEM, IN_VMEM, IN_VMEM],
        out_specs=IN_VMEM,
        out_shape=jax.ShapeDtypeStruct((NCO, rows, cols // NCO), BF16),
        compiler_params=params(),
        cost_estimate=cost(),
        name="pack_patches",
    )(core, own, got)


def spread_kernel(own_ref, beyond_ref, out_ref):
    for x in range(NX):
        out_ref[x, 0] = own_ref[...]
        out_ref[x, 1] = beyond_ref[...]


def spread_patches(own, beyond):
    return pl.pallas_call(
        spread_kernel,
        out_shape=jax.ShapeDtypeStruct((NX, NZH) + own.shape, BF16),
        compiler_params=params(),
        cost_estimate=cost(),
        name="spread_patches",
    )(own, beyond)


def norm_of(patch):
    inv_rms = lax.rsqrt(jnp.mean(patch * patch, axis=-1, keepdims=True) + EPS)
    return patch * inv_rms, inv_rms


def gain_kernel(place, grad_ref, patch_ref, out_ref):
    width = out_ref.shape[1]
    terms = jnp.zeros((1, width), F32)
    for x in range(NX):
        for k in range(NZH):
            z = place[0] if k == 0 else 1 - place[0]
            for c in range(NCO):
                for p in range(grad_ref.shape[4] // width):
                    cols = pl.ds(p * width, width)
                    normed, _ = norm_of(patch_ref[x, k, c, :, cols].astype(F32))
                    grad = grad_ref[x, c, z, :, cols].astype(F32)
                    terms += jnp.sum(grad * normed, axis=0, keepdims=True)
    out_ref[...] = terms


def gain_terms(grads, patches, place, width):
    return pl.pallas_call(
        gain_kernel,
        in_specs=[IN_SMEM] + [IN_VMEM] * 2,
        out_specs=IN_VMEM,
        out_shape=jax.ShapeDtypeStruct((1, width), F32),
        compiler_params=params(),
        cost_estimate=cost(LONG),
        name="gain_terms",
    )(place, grads, patches)


def norm_kernel(place, v_ref, got_ref, patch_ref, gain_ref, out_ref):
    width = gain_ref.shape[1]
    gain = gain_ref[...]
    z = place[0]
    in_half = patch_ref.shape[1] // width // NCO
    for p in range(patch_ref.shape[1] // width):
        c, q = p // in_half, pl.ds(p % in_half * width, width)
        cols = pl.ds(p * width, width)
        owner = got_ref[c, :, q].astype(F32)
        for x in range(NX):
            owner += v_ref[NCO * x + c, z, :, q].astype(F32)
        normed, inv_rms = norm_of(patch_ref[:, cols].astype(F32))
        scaled = owner * gain
        inner = jnp.mean(scaled * normed, axis=-1, keepdims=True)
        out_ref[:, cols] = (inv_rms * (scaled - normed * inner)).astype(BF16)


def norm_part(parts, got, patch_in, norm_gain, place):
    return pl.pallas_call(
        norm_kernel,
        in_specs=[IN_SMEM] + [IN_VMEM] * 4,
        out_specs=IN_VMEM,
        out_shape=jax.ShapeDtypeStruct(patch_in.shape, BF16),
        compiler_params=params(),
        cost_estimate=cost(LONG),
        name="norm_part",
    )(place, parts, got, patch_in, norm_gain.reshape(1, -1))


def sum_over(terms, axes, count):
    rows = jnp.broadcast_to(terms[None], (count,) + terms.shape)
    return jnp.sum(lax.all_to_all(rows, axes, 0, 0, tiled=True), axis=0)


def local(grad_tokens, pre_act, w_fc1, w_fc2, patch_in, norm_gain, owner_pos):
    zh = lax.axis_index("zh").astype(jnp.int32)
    co = lax.axis_index("co").astype(jnp.int32)
    ctx = NX * NZH * NCO
    own, depth = grad_tokens.shape
    group = own * ctx
    slope = gelu_slope(pre_act.astype(F32))
    far_z, near_z, core = (1 - zh).reshape(1), zh.reshape(1), co.reshape(1)
    half = patch_in.shape[1] // NCO
    with jax.named_scope("tokens"):
        outgoing = grad_tokens.reshape(own, ctx, depth // ctx).transpose(1, 0, 2)
        tokens = lax.all_to_all(outgoing, CTX, 0, 0, tiled=True).reshape(group, depth // ctx)
        beside = swap(patch_in, "co")
        tokens, beside = lax.optimization_barrier((tokens, beside))
        tokens = (tokens, swap(tokens, "co"))
    with jax.named_scope("weights"):
        weights_2 = (w_fc2, swap(w_fc2, "co"))
        w_fc1_t = w_fc1.T

    with jax.named_scope("patches"):
        patches = pack_patches(patch_in, beside, core)

    def tie(value, first):
        return lax.optimization_barrier((value, first))[0]

    with jax.named_scope("hidden"):
        sums = hidden_part(weights_2, tokens, core)
        parts = lax.all_to_all(sums, "x", 0, 0, tiled=True)
        ready = tie(patches, sums)
        weights_1 = (w_fc1_t, swap(w_fc1_t, "co"))
        beyond = swap(ready, "zh")
        far = sum_parts(parts, far_z)
        got = widen(swap(far, "zh"))
        around = spread_patches(tie(patches, far), beyond)
        around = lax.all_to_all(around, "x", 0, 0, tiled=True)
    with jax.named_scope("merged"):
        act = act_rows(parts, got, slope, owner_pos, near_z)
        sums = merged_part((act, swap(act, "co")), weights_1, core)
        parts = lax.all_to_all(
            sums.reshape(NX * NCO, NZH * own, half), ("x", "co"), 0, 0, tiled=True
        ).reshape(NX * NCO, NZH, own, half)
        terms = gain_terms(sums, around, near_z, norm_gain.shape[0]).reshape(-1, 128)
        terms = lax.psum(terms, "y")
        parts, terms = lax.optimization_barrier((parts, terms))
        far = sum_halves(parts, far_z)
        got = swap(far, "zh")
    with jax.named_scope("gain"):
        terms = sum_over(tie(terms, far), ("zl", "zh"), NZL * NZH)
    with jax.named_scope("norm"):
        patch_grad = norm_part(parts, got, patch_in, norm_gain, near_z)
    with jax.named_scope("gain"):
        terms = sum_over(terms, ("x", "co"), NX * NCO)
        gain_grad = terms.reshape(-1) / (NY * NZL * ctx)
    return (patch_grad, gain_grad)


def solution(mesh):
    fine = Mesh(mesh.devices.reshape(NY, NZL, NX, NZH, NCO), AXES)
    return jax.shard_map(
        local,
        mesh=fine,
        in_specs=(
            P(DP + CTX, None),
            P(CTX, DP),
            P(None, CTX),
            P(None, CTX),
            P(DP + CTX, None),
            P(),
            P(DP),
        ),
        out_specs=(P(DP + CTX, None), P()),
        check_vma=False,
    )
```

```python
import functools

import jax
import jax.numpy as jnp
from jax import lax
from jax.experimental import pallas as pl
from jax.experimental.pallas import tpu as pltpu
from jax.sharding import Mesh
from jax.sharding import PartitionSpec as P

NY, NZL, NX, NZH, NCO = 8, 6, 4, 2, 2
AXES = ("y", "zl", "x", "zh", "co")
DP = ("y", "zl")
CTX = ("x", "zh", "co")
EPS = 1e-06
F32 = jnp.float32
BF16 = jnp.bfloat16


def gelu_slope(values):
    normal_cdf = 0.5 * (1.0 + lax.erf(values * 0.7071067811865476))
    density = jnp.exp(-0.5 * values * values) * 0.3989422804014327
    return normal_cdf + values * density


def params(mib=12):
    return pltpu.CompilerParams(vmem_limit_bytes=mib * 1024 * 1024)


def cost(flops=1):
    return pl.CostEstimate(flops=flops, bytes_accessed=1, transcendentals=0)


LONG = 20_000_000_000
ANYWHERE = pl.BlockSpec(memory_space=pl.ANY)
IN_VMEM = pl.BlockSpec(memory_space=pltpu.VMEM)
IN_SMEM = pl.BlockSpec(memory_space=pltpu.SMEM)


def swap(value, axis):
    return lax.ppermute(value, axis, [(0, 1), (1, 0)])


def hidden_kernel(core, own_w, got_w, own_t, got_t, out_ref):
    depth = own_t.shape[1]
    total = None
    for w_ref, t_ref in ((own_w, own_t), (got_w, got_t)):
        term = lax.dot_general(
            w_ref[...].reshape(-1, depth),
            t_ref[...],
            (((1,), (1,)), ((), ())),
            preferred_element_type=F32,
        )
        total = term if total is None else total + term
    out_ref[...] = total.astype(BF16).reshape(out_ref.shape)


def hidden_part(weights, tokens, core):
    rows, depth = weights[0].shape
    units = rows // (NX * NZH * NCO)
    count = tokens[0].shape[0]
    weights = [w.reshape(NX, NZH, NCO, units, depth) for w in weights]
    w_spec = pl.BlockSpec((1, NZH, 1, units, depth), lambda i, s: (i, 0, s[0], 0, 0))
    t_spec = pl.BlockSpec((count, depth), lambda i, s: (0, 0))
    return pl.pallas_call(
        hidden_kernel,
        grid_spec=pltpu.PrefetchScalarGridSpec(
            num_scalar_prefetch=1,
            grid=(NX,),
            in_specs=[w_spec, w_spec, t_spec, t_spec],
            out_specs=pl.BlockSpec((1, NZH, units, count), lambda i, s: (i, 0, 0, 0)),
        ),
        out_shape=jax.ShapeDtypeStruct((NX, NZH, units, count), BF16),
        compiler_params=params(52),
        cost_estimate=cost(),
        name="hidden_part",
    )(core, *weights, *tokens)


def total_of(ref, z):
    total = ref[0, z].astype(F32)
    for i in range(1, ref.shape[0]):
        total += ref[i, z].astype(F32)
    return total


def sum_kernel(place, v_ref, out_ref):
    out_ref[...] = total_of(v_ref, place[0]).astype(BF16)


def sum_parts(parts, place):
    return pl.pallas_call(
        sum_kernel,
        in_specs=[IN_SMEM, IN_VMEM],
        out_specs=IN_VMEM,
        out_shape=jax.ShapeDtypeStruct(parts.shape[2:], BF16),
        compiler_params=params(),
        cost_estimate=cost(),
        name="sum_parts",
    )(place, parts)


def wide_kernel(v_ref, out_ref):
    out_ref[...] = v_ref[...].astype(F32)


def widen(value):
    return pl.pallas_call(
        wide_kernel,
        out_shape=jax.ShapeDtypeStruct(value.shape, F32),
        compiler_params=params(),
        cost_estimate=cost(LONG),
        name="widen",
    )(value)


def act_kernel(place, v_ref, got_ref, slope_ref, pos_ref, out_ref):
    act = ((total_of(v_ref, place[0]) + got_ref[...]) * slope_ref[...]).astype(BF16)
    count = act.shape[1]
    pick = (lax.broadcasted_iota(jnp.int32, (count, count), 0) == pos_ref[...]).astype(F32)
    pick = pick.T.astype(BF16)
    moved = lax.dot_general(pick, act, (((1,), (1,)), ((), ())), preferred_element_type=F32)
    moved = moved.astype(BF16)
    own = out_ref.shape[3]
    for x in range(NX):
        for z in range(NZH):
            for c in range(NCO):
                first = ((x * NZH + z) * NCO + c) * own
                out_ref[x, c, z] = moved[first : first + own]


def act_rows(parts, got, slope, owner_pos, place):
    units, count = got.shape
    return pl.pallas_call(
        act_kernel,
        in_specs=[IN_SMEM] + [IN_VMEM] * 4,
        out_specs=IN_VMEM,
        out_shape=jax.ShapeDtypeStruct((NX, NCO, NZH, count // (NX * NCO * NZH), units), BF16),
        compiler_params=params(),
        cost_estimate=cost(),
        name="act_rows",
    )(place, parts, got, slope, owner_pos.reshape(1, count))


def merged_kernel(place, own_a, got_a, own_w, got_w, out_ref):
    depth = own_w.shape[0]
    total = None
    for a_ref, w_ref in ((own_a, own_w), (got_a, got_w)):
        term = lax.dot_general(
            a_ref[...].reshape(-1, depth),
            w_ref[...],
            (((1,), (0,)), ((), ())),
            preferred_element_type=F32,
        )
        total = term if total is None else total + term
    out_ref[...] = total.astype(BF16).reshape(out_ref.shape)


def merged_part(acts, weights, core):
    depth = acts[0].shape[-1]
    cols = weights[0].shape[1] // NCO
    steps = 2
    a_spec = pl.BlockSpec(acts[0].shape, lambda i, s: (0, 0, 0, 0, 0))
    w_spec = pl.BlockSpec((depth, cols // steps), lambda i, s: (0, s[0] * steps + i))
    shape = acts[0].shape[:-1]
    return pl.pallas_call(
        merged_kernel,
        grid_spec=pltpu.PrefetchScalarGridSpec(
            num_scalar_prefetch=1,
            grid=(steps,),
            in_specs=[a_spec, a_spec, w_spec, w_spec],
            out_specs=pl.BlockSpec(shape + (cols // steps,), lambda i, s: (0, 0, 0, 0, i)),
        ),
        out_shape=jax.ShapeDtypeStruct(shape + (cols,), BF16),
        compiler_params=params(),
        cost_estimate=cost(),
        name="merged_part",
    )(core, *acts, *weights)


def halves_kernel(place, v_ref, out_ref):
    z = place[0]
    for c in range(NCO):
        total = v_ref[c, z].astype(F32)
        for x in range(1, NX):
            total += v_ref[NCO * x + c, z].astype(F32)
        out_ref[c] = total.astype(BF16)


def sum_halves(parts, place):
    return pl.pallas_call(
        halves_kernel,
        in_specs=[IN_SMEM, IN_VMEM],
        out_specs=IN_VMEM,
        out_shape=jax.ShapeDtypeStruct((NCO,) + parts.shape[2:], BF16),
        compiler_params=params(),
        cost_estimate=cost(),
        name="sum_halves",
    )(place, parts)


def pack_kernel(core, own_ref, got_ref, out_ref):
    half = out_ref.shape[2]
    cols = pl.ds(pl.multiple_of(core[0] * half, 128), half)
    out_ref[core[0]] = own_ref[:, cols]
    out_ref[1 - core[0]] = got_ref[:, cols]


def pack_patches(own, got, core):
    rows, cols = own.shape
    return pl.pallas_call(
        pack_kernel,
        in_specs=[IN_SMEM, IN_VMEM, IN_VMEM],
        out_specs=IN_VMEM,
        out_shape=jax.ShapeDtypeStruct((NCO, rows, cols // NCO), BF16),
        compiler_params=params(),
        cost_estimate=cost(),
        name="pack_patches",
    )(core, own, got)


def spread_kernel(own_ref, out_ref):
    for x in range(NX):
        out_ref[x] = own_ref[...]


def spread_patches(own):
    return pl.pallas_call(
        spread_kernel,
        out_shape=jax.ShapeDtypeStruct((NX,) + own.shape, BF16),
        compiler_params=params(),
        cost_estimate=cost(),
        name="spread_patches",
    )(own)


def norm_of(patch):
    inv_rms = lax.rsqrt(jnp.mean(patch * patch, axis=-1, keepdims=True) + EPS)
    return patch * inv_rms, inv_rms


def gain_kernel(place, grad_ref, beyond_ref, *refs):
    out_ref = refs[-1]
    width = out_ref.shape[1]
    terms = jnp.zeros((1, width), F32)
    for k in range(NX):
        here = (lax.rem(place[1] + k, NX), place[0], refs[k])
        there = (k, 1 - place[0], beyond_ref.at[k])
        for x, z, patch_ref in (here, there):
            for c in range(NCO):
                for p in range(grad_ref.shape[4] // width):
                    cols = pl.ds(p * width, width)
                    normed, _ = norm_of(patch_ref[c, :, cols].astype(F32))
                    grad = grad_ref[x, c, z, :, cols].astype(F32)
                    terms += jnp.sum(grad * normed, axis=0, keepdims=True)
    out_ref[...] = terms


def gain_terms(grads, beyond, around, place, width):
    return pl.pallas_call(
        gain_kernel,
        in_specs=[IN_SMEM] + [IN_VMEM] * (2 + NX),
        out_specs=IN_VMEM,
        out_shape=jax.ShapeDtypeStruct((1, width), F32),
        compiler_params=params(),
        cost_estimate=cost(LONG),
        name="gain_terms",
    )(place, grads, beyond, *around)


def norm_kernel(place, v_ref, got_ref, patch_ref, gain_ref, out_ref):
    width = gain_ref.shape[1]
    gain = gain_ref[...]
    z = place[0]
    in_half = patch_ref.shape[1] // width // NCO
    for p in range(patch_ref.shape[1] // width):
        c, q = p // in_half, pl.ds(p % in_half * width, width)
        cols = pl.ds(p * width, width)
        owner = got_ref[c, :, q].astype(F32)
        for x in range(NX):
            owner += v_ref[NCO * x + c, z, :, q].astype(F32)
        normed, inv_rms = norm_of(patch_ref[:, cols].astype(F32))
        scaled = owner * gain
        inner = jnp.mean(scaled * normed, axis=-1, keepdims=True)
        out_ref[:, cols] = (inv_rms * (scaled - normed * inner)).astype(BF16)


def norm_part(parts, got, patch_in, norm_gain, place):
    return pl.pallas_call(
        norm_kernel,
        in_specs=[IN_SMEM] + [IN_VMEM] * 4,
        out_specs=IN_VMEM,
        out_shape=jax.ShapeDtypeStruct(patch_in.shape, BF16),
        compiler_params=params(),
        cost_estimate=cost(LONG),
        name="norm_part",
    )(place, parts, got, patch_in, norm_gain.reshape(1, -1))


def sum_over(terms, axes, count):
    rows = jnp.broadcast_to(terms[None], (count,) + terms.shape)
    return jnp.sum(lax.all_to_all(rows, axes, 0, 0, tiled=True), axis=0)


def local(grad_tokens, pre_act, w_fc1, w_fc2, patch_in, norm_gain, owner_pos):
    zh = lax.axis_index("zh").astype(jnp.int32)
    co = lax.axis_index("co").astype(jnp.int32)
    ctx = NX * NZH * NCO
    own, depth = grad_tokens.shape
    group = own * ctx
    slope = gelu_slope(pre_act.astype(F32))
    far_z, near_z, core = (1 - zh).reshape(1), zh.reshape(1), co.reshape(1)
    half = patch_in.shape[1] // NCO
    with jax.named_scope("tokens"):
        outgoing = grad_tokens.reshape(own, ctx, depth // ctx).transpose(1, 0, 2)
        tokens = lax.all_to_all(outgoing, CTX, 0, 0, tiled=True).reshape(group, depth // ctx)
        beside = swap(patch_in, "co")
        patches = pack_patches(patch_in, beside, core)
        around = [
            lax.ppermute(patches, "x", [(i, (i - d) % NX) for i in range(NX)]) for d in (1, 2, 3)
        ]
        tokens, around = lax.optimization_barrier((tokens, around))
        tokens = (tokens, swap(tokens, "co"))
    with jax.named_scope("weights"):
        weights_2 = (w_fc2, swap(w_fc2, "co"))
        w_fc1_t = w_fc1.T

    def tie(value, first):
        return lax.optimization_barrier((value, first))[0]

    with jax.named_scope("hidden"):
        sums = hidden_part(weights_2, tokens, core)
        parts = lax.all_to_all(sums, "x", 0, 0, tiled=True)
        ready = tie(patches, sums)
        weights_1 = (w_fc1_t, swap(w_fc1_t, "co"))
        beyond = swap(ready, "zh")
        far = sum_parts(parts, far_z)
        got = widen(swap(far, "zh"))
        beyond = spread_patches(tie(beyond, far))
        beyond = lax.all_to_all(beyond, "x", 0, 0, tiled=True)
    with jax.named_scope("merged"):
        act = act_rows(parts, got, slope, owner_pos, near_z)
        sums = merged_part((act, swap(act, "co")), weights_1, core)
        parts = lax.all_to_all(
            sums.reshape(NX * NCO, NZH * own, half), ("x", "co"), 0, 0, tiled=True
        ).reshape(NX * NCO, NZH, own, half)
        here = jnp.stack([zh, lax.axis_index("x").astype(jnp.int32)])
        terms = gain_terms(sums, beyond, [patches] + around, here, norm_gain.shape[0]).reshape(-1, 128)
        terms = lax.psum(terms, "y")
        parts, terms = lax.optimization_barrier((parts, terms))
        far = sum_halves(parts, far_z)
        got = swap(far, "zh")
    with jax.named_scope("gain"):
        terms = sum_over(tie(terms, far), ("zl", "zh"), NZL * NZH)
    with jax.named_scope("norm"):
        patch_grad = norm_part(parts, got, patch_in, norm_gain, near_z)
    with jax.named_scope("gain"):
        terms = sum_over(terms, ("x", "co"), NX * NCO)
        gain_grad = terms.reshape(-1) / (NY * NZL * ctx)
    return (patch_grad, gain_grad)


def solution(mesh):
    fine = Mesh(mesh.devices.reshape(NY, NZL, NX, NZH, NCO), AXES)
    return jax.shard_map(
        local,
        mesh=fine,
        in_specs=(
            P(DP + CTX, None),
            P(CTX, DP),
            P(None, CTX),
            P(None, CTX),
            P(DP + CTX, None),
            P(),
            P(DP),
        ),
        out_specs=(P(DP + CTX, None), P()),
        check_vma=False,
    )
```

```python
import functools

import jax
import jax.numpy as jnp
from jax import lax
from jax.experimental import pallas as pl
from jax.experimental.pallas import tpu as pltpu
from jax.sharding import Mesh
from jax.sharding import PartitionSpec as P

NY, NZL, NX, NZH, NCO = 8, 6, 4, 2, 2
AXES = ("y", "zl", "x", "zh", "co")
DP = ("y", "zl")
CTX = ("x", "zh", "co")
EPS = 1e-06
F32 = jnp.float32
BF16 = jnp.bfloat16


def gelu_slope(values):
    normal_cdf = 0.5 * (1.0 + lax.erf(values * 0.7071067811865476))
    density = jnp.exp(-0.5 * values * values) * 0.3989422804014327
    return normal_cdf + values * density


def params(mib=12):
    return pltpu.CompilerParams(vmem_limit_bytes=mib * 1024 * 1024)


def cost(flops=1):
    return pl.CostEstimate(flops=flops, bytes_accessed=1, transcendentals=0)


LONG = 20_000_000_000
ANYWHERE = pl.BlockSpec(memory_space=pl.ANY)
IN_VMEM = pl.BlockSpec(memory_space=pltpu.VMEM)
IN_SMEM = pl.BlockSpec(memory_space=pltpu.SMEM)


def swap(value, axis):
    return lax.ppermute(value, axis, [(0, 1), (1, 0)])


def hidden_kernel(core, own_w, got_w, own_t, got_t, out_ref):
    depth = own_t.shape[1]
    total = None
    for w_ref, t_ref in ((own_w, own_t), (got_w, got_t)):
        term = lax.dot_general(
            w_ref[...].reshape(-1, depth),
            t_ref[...],
            (((1,), (1,)), ((), ())),
            preferred_element_type=F32,
        )
        total = term if total is None else total + term
    out_ref[...] = total.astype(BF16).reshape(out_ref.shape)


def hidden_part(weights, tokens, core):
    rows, depth = weights[0].shape
    units = rows // (NX * NZH * NCO)
    count = tokens[0].shape[0]
    weights = [w.reshape(NX, NZH, NCO, units, depth) for w in weights]
    w_spec = pl.BlockSpec((1, NZH, 1, units, depth), lambda i, s: (i, 0, s[0], 0, 0))
    t_spec = pl.BlockSpec((count, depth), lambda i, s: (0, 0))
    return pl.pallas_call(
        hidden_kernel,
        grid_spec=pltpu.PrefetchScalarGridSpec(
            num_scalar_prefetch=1,
            grid=(NX,),
            in_specs=[w_spec, w_spec, t_spec, t_spec],
            out_specs=pl.BlockSpec((1, NZH, units, count), lambda i, s: (i, 0, 0, 0)),
        ),
        out_shape=jax.ShapeDtypeStruct((NX, NZH, units, count), BF16),
        compiler_params=params(52),
        cost_estimate=cost(),
        name="hidden_part",
    )(core, *weights, *tokens)


def total_of(ref, z):
    total = ref[0, z].astype(F32)
    for i in range(1, ref.shape[0]):
        total += ref[i, z].astype(F32)
    return total


def sum_kernel(place, v_ref, out_ref):
    out_ref[...] = total_of(v_ref, place[0]).astype(BF16)


def sum_parts(parts, place):
    return pl.pallas_call(
        sum_kernel,
        in_specs=[IN_SMEM, IN_VMEM],
        out_specs=IN_VMEM,
        out_shape=jax.ShapeDtypeStruct(parts.shape[2:], BF16),
        compiler_params=params(),
        cost_estimate=cost(),
        name="sum_parts",
    )(place, parts)


def wide_kernel(v_ref, out_ref):
    out_ref[...] = v_ref[...].astype(F32)


def widen(value):
    return pl.pallas_call(
        wide_kernel,
        out_shape=jax.ShapeDtypeStruct(value.shape, F32),
        compiler_params=params(),
        cost_estimate=cost(LONG),
        name="widen",
    )(value)


def act_kernel(place, v_ref, got_ref, slope_ref, pos_ref, out_ref):
    act = ((total_of(v_ref, place[0]) + got_ref[...]) * slope_ref[...]).astype(BF16)
    count = act.shape[1]
    pick = (lax.broadcasted_iota(jnp.int32, (count, count), 0) == pos_ref[...]).astype(F32)
    pick = pick.T.astype(BF16)
    moved = lax.dot_general(pick, act, (((1,), (1,)), ((), ())), preferred_element_type=F32)
    moved = moved.astype(BF16)
    own = out_ref.shape[3]
    for x in range(NX):
        for z in range(NZH):
            for c in range(NCO):
                first = ((x * NZH + z) * NCO + c) * own
                out_ref[x, c, z] = moved[first : first + own]


def act_rows(parts, got, slope, owner_pos, place):
    units, count = got.shape
    return pl.pallas_call(
        act_kernel,
        in_specs=[IN_SMEM] + [IN_VMEM] * 4,
        out_specs=IN_VMEM,
        out_shape=jax.ShapeDtypeStruct((NX, NCO, NZH, count // (NX * NCO * NZH), units), BF16),
        compiler_params=params(),
        cost_estimate=cost(),
        name="act_rows",
    )(place, parts, got, slope, owner_pos.reshape(1, count))


def merged_kernel(place, own_a, got_a, own_w, got_w, out_ref):
    depth = own_w.shape[0]
    total = None
    for a_ref, w_ref in ((own_a, own_w), (got_a, got_w)):
        term = lax.dot_general(
            a_ref[...].reshape(-1, depth),
            w_ref[...],
            (((1,), (0,)), ((), ())),
            preferred_element_type=F32,
        )
        total = term if total is None else total + term
    out_ref[...] = total.astype(BF16).reshape(out_ref.shape)


def merged_part(acts, weights, core):
    depth = acts[0].shape[-1]
    cols = weights[0].shape[1] // NCO
    steps = 2
    a_spec = pl.BlockSpec(acts[0].shape, lambda i, s: (0, 0, 0, 0, 0))
    w_spec = pl.BlockSpec((depth, cols // steps), lambda i, s: (0, s[0] * steps + i))
    shape = acts[0].shape[:-1]
    return pl.pallas_call(
        merged_kernel,
        grid_spec=pltpu.PrefetchScalarGridSpec(
            num_scalar_prefetch=1,
            grid=(steps,),
            in_specs=[a_spec, a_spec, w_spec, w_spec],
            out_specs=pl.BlockSpec(shape + (cols // steps,), lambda i, s: (0, 0, 0, 0, i)),
        ),
        out_shape=jax.ShapeDtypeStruct(shape + (cols,), BF16),
        compiler_params=params(),
        cost_estimate=cost(),
        name="merged_part",
    )(core, *acts, *weights)


def halves_kernel(place, v_ref, out_ref):
    z = place[0]
    for c in range(NCO):
        total = v_ref[c, z].astype(F32)
        for x in range(1, NX):
            total += v_ref[NCO * x + c, z].astype(F32)
        out_ref[c] = total.astype(BF16)


def sum_halves(parts, place):
    return pl.pallas_call(
        halves_kernel,
        in_specs=[IN_SMEM, IN_VMEM],
        out_specs=IN_VMEM,
        out_shape=jax.ShapeDtypeStruct((NCO,) + parts.shape[2:], BF16),
        compiler_params=params(),
        cost_estimate=cost(),
        name="sum_halves",
    )(place, parts)


def pack_kernel(core, own_ref, got_ref, out_ref):
    half = out_ref.shape[2]
    cols = pl.ds(pl.multiple_of(core[0] * half, 128), half)
    out_ref[core[0]] = own_ref[:, cols]
    out_ref[1 - core[0]] = got_ref[:, cols]


def pack_patches(own, got, core):
    rows, cols = own.shape
    return pl.pallas_call(
        pack_kernel,
        in_specs=[IN_SMEM, IN_VMEM, IN_VMEM],
        out_specs=IN_VMEM,
        out_shape=jax.ShapeDtypeStruct((NCO, rows, cols // NCO), BF16),
        compiler_params=params(),
        cost_estimate=cost(),
        name="pack_patches",
    )(core, own, got)


def norm_of(patch):
    inv_rms = lax.rsqrt(jnp.mean(patch * patch, axis=-1, keepdims=True) + EPS)
    return patch * inv_rms, inv_rms


def gain_kernel(place, grad_ref, *refs):
    out_ref = refs[-1]
    width = out_ref.shape[1]
    terms = jnp.zeros((1, width), F32)
    for shift, patch_ref in enumerate(refs[:-1]):
        x = lax.rem(place[0] + shift, NX)
        for k in range(NZH):
            z = place[1] if k == 0 else 1 - place[1]
            for c in range(NCO):
                for p in range(grad_ref.shape[4] // width):
                    cols = pl.ds(p * width, width)
                    normed, _ = norm_of(patch_ref[k, c, :, cols].astype(F32))
                    grad = grad_ref[x, c, z, :, cols].astype(F32)
                    terms += jnp.sum(grad * normed, axis=0, keepdims=True)
    out_ref[...] = terms


def gain_terms(grads, patches, place, width):
    return pl.pallas_call(
        gain_kernel,
        in_specs=[IN_SMEM] + [IN_VMEM] * (1 + NX),
        out_specs=IN_VMEM,
        out_shape=jax.ShapeDtypeStruct((1, width), F32),
        compiler_params=params(),
        cost_estimate=cost(LONG),
        name="gain_terms",
    )(place, grads, *patches)


def norm_kernel(place, v_ref, got_ref, patch_ref, gain_ref, out_ref):
    width = gain_ref.shape[1]
    gain = gain_ref[...]
    z = place[0]
    in_half = patch_ref.shape[1] // width // NCO
    for p in range(patch_ref.shape[1] // width):
        c, q = p // in_half, pl.ds(p % in_half * width, width)
        cols = pl.ds(p * width, width)
        owner = got_ref[c, :, q].astype(F32)
        for x in range(NX):
            owner += v_ref[NCO * x + c, z, :, q].astype(F32)
        normed, inv_rms = norm_of(patch_ref[:, cols].astype(F32))
        scaled = owner * gain
        inner = jnp.mean(scaled * normed, axis=-1, keepdims=True)
        out_ref[:, cols] = (inv_rms * (scaled - normed * inner)).astype(BF16)


def norm_part(parts, got, patch_in, norm_gain, place):
    return pl.pallas_call(
        norm_kernel,
        in_specs=[IN_SMEM] + [IN_VMEM] * 4,
        out_specs=IN_VMEM,
        out_shape=jax.ShapeDtypeStruct(patch_in.shape, BF16),
        compiler_params=params(),
        cost_estimate=cost(LONG),
        name="norm_part",
    )(place, parts, got, patch_in, norm_gain.reshape(1, -1))


def sum_over(terms, axes, count):
    rows = jnp.broadcast_to(terms[None], (count,) + terms.shape)
    return jnp.sum(lax.all_to_all(rows, axes, 0, 0, tiled=True), axis=0)


def local(grad_tokens, pre_act, w_fc1, w_fc2, patch_in, norm_gain, owner_pos):
    zh = lax.axis_index("zh").astype(jnp.int32)
    co = lax.axis_index("co").astype(jnp.int32)
    ctx = NX * NZH * NCO
    own, depth = grad_tokens.shape
    group = own * ctx
    slope = gelu_slope(pre_act.astype(F32))
    far_z, near_z, core = (1 - zh).reshape(1), zh.reshape(1), co.reshape(1)
    half = patch_in.shape[1] // NCO
    with jax.named_scope("tokens"):
        outgoing = grad_tokens.reshape(own, ctx, depth // ctx).transpose(1, 0, 2)
        tokens = lax.all_to_all(outgoing, CTX, 0, 0, tiled=True).reshape(group, depth // ctx)
        beside = swap(patch_in, "co")
        tokens, beside = lax.optimization_barrier((tokens, beside))
        tokens = (tokens, swap(tokens, "co"))
    with jax.named_scope("weights"):
        weights_2 = (w_fc2, swap(w_fc2, "co"))
        w_fc1_t = w_fc1.T

    with jax.named_scope("patches"):
        patches = pack_patches(patch_in, beside, core)

    def tie(value, first):
        return lax.optimization_barrier((value, first))[0]

    with jax.named_scope("hidden"):
        sums = hidden_part(weights_2, tokens, core)
        parts = lax.all_to_all(sums, "x", 0, 0, tiled=True)
        ready = tie(patches, sums)
        weights_1 = (w_fc1_t, swap(w_fc1_t, "co"))
        beyond = swap(ready, "zh")
        far = sum_parts(parts, far_z)
        got = widen(swap(far, "zh"))
        patches = jnp.stack([tie(patches, far), beyond])
        around = [patches] + [
            lax.ppermute(patches, "x", [(i, (i - d) % NX) for i in range(NX)]) for d in (1, 2, 3)
        ]
    with jax.named_scope("merged"):
        act = act_rows(parts, got, slope, owner_pos, near_z)
        sums = merged_part((act, swap(act, "co")), weights_1, core)
        parts = lax.all_to_all(
            sums.reshape(NX * NCO, NZH * own, half), ("x", "co"), 0, 0, tiled=True
        ).reshape(NX * NCO, NZH, own, half)
        here = jnp.stack([lax.axis_index("x").astype(jnp.int32), zh])
        terms = gain_terms(sums, around, here, norm_gain.shape[0]).reshape(-1, 128)
        terms = lax.psum(terms, "y")
        parts, terms = lax.optimization_barrier((parts, terms))
        far = sum_halves(parts, far_z)
        got = swap(far, "zh")
    with jax.named_scope("gain"):
        terms = sum_over(tie(terms, far), ("zl", "zh"), NZL * NZH)
    with jax.named_scope("norm"):
        patch_grad = norm_part(parts, got, patch_in, norm_gain, near_z)
    with jax.named_scope("gain"):
        terms = sum_over(terms, ("x", "co"), NX * NCO)
        gain_grad = terms.reshape(-1) / (NY * NZL * ctx)
    return (patch_grad, gain_grad)


def solution(mesh):
    fine = Mesh(mesh.devices.reshape(NY, NZL, NX, NZH, NCO), AXES)
    return jax.shard_map(
        local,
        mesh=fine,
        in_specs=(
            P(DP + CTX, None),
            P(CTX, DP),
            P(None, CTX),
            P(None, CTX),
            P(DP + CTX, None),
            P(),
            P(DP),
        ),
        out_specs=(P(DP + CTX, None), P()),
        check_vma=False,
    )
```

```python
import functools

import jax
import jax.numpy as jnp
from jax import lax
from jax.experimental import pallas as pl
from jax.experimental.pallas import tpu as pltpu
from jax.sharding import Mesh
from jax.sharding import PartitionSpec as P

NY, NZL, NX, NZH, NCO = 8, 6, 4, 2, 2
AXES = ("y", "zl", "x", "zh", "co")
DP = ("y", "zl")
CTX = ("x", "zh", "co")
EPS = 1e-06
F32 = jnp.float32
BF16 = jnp.bfloat16


def gelu_slope(values):
    normal_cdf = 0.5 * (1.0 + lax.erf(values * 0.7071067811865476))
    density = jnp.exp(-0.5 * values * values) * 0.3989422804014327
    return normal_cdf + values * density


def params(mib=12):
    return pltpu.CompilerParams(vmem_limit_bytes=mib * 1024 * 1024)


def cost(flops=1):
    return pl.CostEstimate(flops=flops, bytes_accessed=1, transcendentals=0)


LONG = 20_000_000_000
ANYWHERE = pl.BlockSpec(memory_space=pl.ANY)
IN_VMEM = pl.BlockSpec(memory_space=pltpu.VMEM)
IN_SMEM = pl.BlockSpec(memory_space=pltpu.SMEM)


def swap(value, axis):
    return lax.ppermute(value, axis, [(0, 1), (1, 0)])


def hidden_kernel(core, own_w, got_w, own_t, got_t, out_ref):
    depth = own_t.shape[1]
    total = None
    for w_ref, t_ref in ((own_w, own_t), (got_w, got_t)):
        term = lax.dot_general(
            w_ref[...].reshape(-1, depth),
            t_ref[...],
            (((1,), (1,)), ((), ())),
            preferred_element_type=F32,
        )
        total = term if total is None else total + term
    out_ref[...] = total.astype(BF16).reshape(out_ref.shape)


def hidden_part(weights, tokens, core):
    rows, depth = weights[0].shape
    units = rows // (NX * NZH * NCO)
    count = tokens[0].shape[0]
    weights = [w.reshape(NX, NZH, NCO, units, depth) for w in weights]
    w_spec = pl.BlockSpec((1, NZH, 1, units, depth), lambda i, s: (i, 0, s[0], 0, 0))
    t_spec = pl.BlockSpec((count, depth), lambda i, s: (0, 0))
    return pl.pallas_call(
        hidden_kernel,
        grid_spec=pltpu.PrefetchScalarGridSpec(
            num_scalar_prefetch=1,
            grid=(NX,),
            in_specs=[w_spec, w_spec, t_spec, t_spec],
            out_specs=pl.BlockSpec((1, NZH, units, count), lambda i, s: (i, 0, 0, 0)),
        ),
        out_shape=jax.ShapeDtypeStruct((NX, NZH, units, count), BF16),
        compiler_params=params(52),
        cost_estimate=cost(),
        name="hidden_part",
    )(core, *weights, *tokens)


def total_of(ref, z):
    total = ref[0, z].astype(F32)
    for i in range(1, ref.shape[0]):
        total += ref[i, z].astype(F32)
    return total


def sum_kernel(place, v_ref, out_ref):
    out_ref[...] = total_of(v_ref, place[0]).astype(BF16)


def sum_parts(parts, place):
    return pl.pallas_call(
        sum_kernel,
        in_specs=[IN_SMEM, IN_VMEM],
        out_specs=IN_VMEM,
        out_shape=jax.ShapeDtypeStruct(parts.shape[2:], BF16),
        compiler_params=params(),
        cost_estimate=cost(),
        name="sum_parts",
    )(place, parts)


def wide_kernel(v_ref, out_ref):
    out_ref[...] = v_ref[...].astype(F32)


def widen(value):
    return pl.pallas_call(
        wide_kernel,
        out_shape=jax.ShapeDtypeStruct(value.shape, F32),
        compiler_params=params(),
        cost_estimate=cost(LONG),
        name="widen",
    )(value)


def act_kernel(place, v_ref, got_ref, slope_ref, pos_ref, out_ref):
    act = ((total_of(v_ref, place[0]) + got_ref[...]) * slope_ref[...]).astype(BF16)
    count = act.shape[1]
    pick = (lax.broadcasted_iota(jnp.int32, (count, count), 0) == pos_ref[...]).astype(F32)
    pick = pick.T.astype(BF16)
    moved = lax.dot_general(pick, act, (((1,), (1,)), ((), ())), preferred_element_type=F32)
    moved = moved.astype(BF16)
    own = out_ref.shape[3]
    for x in range(NX):
        for z in range(NZH):
            for c in range(NCO):
                first = ((x * NZH + z) * NCO + c) * own
                out_ref[x, c, z] = moved[first : first + own]


def act_rows(parts, got, slope, owner_pos, place):
    units, count = got.shape
    return pl.pallas_call(
        act_kernel,
        in_specs=[IN_SMEM] + [IN_VMEM] * 4,
        out_specs=IN_VMEM,
        out_shape=jax.ShapeDtypeStruct((NX, NCO, NZH, count // (NX * NCO * NZH), units), BF16),
        compiler_params=params(),
        cost_estimate=cost(),
        name="act_rows",
    )(place, parts, got, slope, owner_pos.reshape(1, count))


def merged_kernel(place, own_a, got_a, own_w, got_w, out_ref):
    depth = own_w.shape[0]
    total = None
    for a_ref, w_ref in ((own_a, own_w), (got_a, got_w)):
        term = lax.dot_general(
            a_ref[...].reshape(-1, depth),
            w_ref[...],
            (((1,), (0,)), ((), ())),
            preferred_element_type=F32,
        )
        total = term if total is None else total + term
    out_ref[...] = total.astype(BF16).reshape(out_ref.shape)


def merged_part(acts, weights, core):
    depth = acts[0].shape[-1]
    cols = weights[0].shape[1] // NCO
    steps = 2
    a_spec = pl.BlockSpec(acts[0].shape, lambda i, s: (0, 0, 0, 0, 0))
    w_spec = pl.BlockSpec((depth, cols // steps), lambda i, s: (0, s[0] * steps + i))
    shape = acts[0].shape[:-1]
    return pl.pallas_call(
        merged_kernel,
        grid_spec=pltpu.PrefetchScalarGridSpec(
            num_scalar_prefetch=1,
            grid=(steps,),
            in_specs=[a_spec, a_spec, w_spec, w_spec],
            out_specs=pl.BlockSpec(shape + (cols // steps,), lambda i, s: (0, 0, 0, 0, i)),
        ),
        out_shape=jax.ShapeDtypeStruct(shape + (cols,), BF16),
        compiler_params=params(52),
        cost_estimate=cost(),
        name="merged_part",
    )(core, *acts, *weights)


def halves_kernel(place, v_ref, out_ref):
    z = place[0]
    for c in range(NCO):
        total = v_ref[c, z].astype(F32)
        for x in range(1, NX):
            total += v_ref[NCO * x + c, z].astype(F32)
        out_ref[c] = total.astype(BF16)


def sum_halves(parts, place):
    return pl.pallas_call(
        halves_kernel,
        in_specs=[IN_SMEM, IN_VMEM],
        out_specs=IN_VMEM,
        out_shape=jax.ShapeDtypeStruct((NCO,) + parts.shape[2:], BF16),
        compiler_params=params(),
        cost_estimate=cost(),
        name="sum_halves",
    )(place, parts)


def pack_kernel(core, own_ref, got_ref, out_ref):
    half = out_ref.shape[2]
    cols = pl.ds(pl.multiple_of(core[0] * half, 128), half)
    out_ref[core[0]] = own_ref[:, cols]
    out_ref[1 - core[0]] = got_ref[:, cols]


def pack_patches(own, got, core):
    rows, cols = own.shape
    return pl.pallas_call(
        pack_kernel,
        in_specs=[IN_SMEM, IN_VMEM, IN_VMEM],
        out_specs=IN_VMEM,
        out_shape=jax.ShapeDtypeStruct((NCO, rows, cols // NCO), BF16),
        compiler_params=params(),
        cost_estimate=cost(),
        name="pack_patches",
    )(core, own, got)


def norm_of(patch):
    inv_rms = lax.rsqrt(jnp.mean(patch * patch, axis=-1, keepdims=True) + EPS)
    return patch * inv_rms, inv_rms


def gain_kernel(place, grad_ref, *refs):
    out_ref = refs[-1]
    width = out_ref.shape[1]
    terms = jnp.zeros((1, width), F32)
    for shift, patch_ref in enumerate(refs[:-1]):
        x = lax.rem(place[0] + shift, NX)
        for k in range(NZH):
            z = place[1] if k == 0 else 1 - place[1]
            for c in range(NCO):
                for p in range(grad_ref.shape[4] // width):
                    cols = pl.ds(p * width, width)
                    normed, _ = norm_of(patch_ref[k, c, :, cols].astype(F32))
                    grad = grad_ref[x, c, z, :, cols].astype(F32)
                    terms += jnp.sum(grad * normed, axis=0, keepdims=True)
    out_ref[...] = terms


def gain_terms(grads, patches, place, width):
    return pl.pallas_call(
        gain_kernel,
        in_specs=[IN_SMEM] + [IN_VMEM] * (1 + NX),
        out_specs=IN_VMEM,
        out_shape=jax.ShapeDtypeStruct((1, width), F32),
        compiler_params=params(),
        cost_estimate=cost(LONG),
        name="gain_terms",
    )(place, grads, *patches)


def norm_kernel(place, v_ref, got_ref, patch_ref, gain_ref, out_ref):
    width = gain_ref.shape[1]
    gain = gain_ref[...]
    z = place[0]
    in_half = patch_ref.shape[1] // width // NCO
    for p in range(patch_ref.shape[1] // width):
        c, q = p // in_half, pl.ds(p % in_half * width, width)
        cols = pl.ds(p * width, width)
        owner = got_ref[c, :, q].astype(F32)
        for x in range(NX):
            owner += v_ref[NCO * x + c, z, :, q].astype(F32)
        normed, inv_rms = norm_of(patch_ref[:, cols].astype(F32))
        scaled = owner * gain
        inner = jnp.mean(scaled * normed, axis=-1, keepdims=True)
        out_ref[:, cols] = (inv_rms * (scaled - normed * inner)).astype(BF16)


def norm_part(parts, got, patch_in, norm_gain, place):
    return pl.pallas_call(
        norm_kernel,
        in_specs=[IN_SMEM] + [IN_VMEM] * 4,
        out_specs=IN_VMEM,
        out_shape=jax.ShapeDtypeStruct(patch_in.shape, BF16),
        compiler_params=params(),
        cost_estimate=cost(LONG),
        name="norm_part",
    )(place, parts, got, patch_in, norm_gain.reshape(1, -1))


def sum_over(terms, axes, count):
    rows = jnp.broadcast_to(terms[None], (count,) + terms.shape)
    return jnp.sum(lax.all_to_all(rows, axes, 0, 0, tiled=True), axis=0)


def local(grad_tokens, pre_act, w_fc1, w_fc2, patch_in, norm_gain, owner_pos):
    zh = lax.axis_index("zh").astype(jnp.int32)
    co = lax.axis_index("co").astype(jnp.int32)
    ctx = NX * NZH * NCO
    own, depth = grad_tokens.shape
    group = own * ctx
    slope = gelu_slope(pre_act.astype(F32))
    far_z, near_z, core = (1 - zh).reshape(1), zh.reshape(1), co.reshape(1)
    half = patch_in.shape[1] // NCO
    with jax.named_scope("tokens"):
        outgoing = grad_tokens.reshape(own, ctx, depth // ctx).transpose(1, 0, 2)
        tokens = lax.all_to_all(outgoing, CTX, 0, 0, tiled=True).reshape(group, depth // ctx)
        beside = swap(patch_in, "co")
        tokens, beside = lax.optimization_barrier((tokens, beside))
        tokens = (tokens, swap(tokens, "co"))
    with jax.named_scope("weights"):
        weights_2 = (w_fc2, swap(w_fc2, "co"))
        w_fc1_t = w_fc1.T

    with jax.named_scope("patches"):
        patches = pack_patches(patch_in, beside, core)

    def tie(value, first):
        return lax.optimization_barrier((value, first))[0]

    with jax.named_scope("hidden"):
        sums = hidden_part(weights_2, tokens, core)
        parts = lax.all_to_all(sums, "x", 0, 0, tiled=True)
        ready = tie(patches, sums)
        weights_1 = (w_fc1_t, swap(w_fc1_t, "co"))
        beyond = swap(ready, "zh")
        far = sum_parts(parts, far_z)
        got = widen(swap(far, "zh"))
        patches = jnp.stack([tie(patches, far), beyond])
        around = [patches] + [
            lax.ppermute(patches, "x", [(i, (i - d) % NX) for i in range(NX)]) for d in (1, 2, 3)
        ]
    with jax.named_scope("merged"):
        act = act_rows(parts, got, slope, owner_pos, near_z)
        sums = merged_part((act, swap(act, "co")), weights_1, core)
        parts = lax.all_to_all(
            sums.reshape(NX * NCO, NZH * own, half), ("x", "co"), 0, 0, tiled=True
        ).reshape(NX * NCO, NZH, own, half)
        here = jnp.stack([lax.axis_index("x").astype(jnp.int32), zh])
        terms = gain_terms(sums, around, here, norm_gain.shape[0]).reshape(-1, 128)
        terms = lax.psum(terms, "y")
        parts, terms = lax.optimization_barrier((parts, terms))
        far = sum_halves(parts, far_z)
        got = swap(far, "zh")
    with jax.named_scope("gain"):
        terms = sum_over(tie(terms, far), ("zl", "zh"), NZL * NZH)
    with jax.named_scope("norm"):
        patch_grad = norm_part(parts, got, patch_in, norm_gain, near_z)
    with jax.named_scope("gain"):
        terms = sum_over(terms, ("x", "co"), NX * NCO)
        gain_grad = terms.reshape(-1) / (NY * NZL * ctx)
    return (patch_grad, gain_grad)


def solution(mesh):
    fine = Mesh(mesh.devices.reshape(NY, NZL, NX, NZH, NCO), AXES)
    return jax.shard_map(
        local,
        mesh=fine,
        in_specs=(
            P(DP + CTX, None),
            P(CTX, DP),
            P(None, CTX),
            P(None, CTX),
            P(DP + CTX, None),
            P(),
            P(DP),
        ),
        out_specs=(P(DP + CTX, None), P()),
        check_vma=False,
    )
```

```python
import functools

import jax
import jax.numpy as jnp
from jax import lax
from jax.experimental import pallas as pl
from jax.experimental.pallas import tpu as pltpu
from jax.sharding import Mesh
from jax.sharding import PartitionSpec as P

NY, NZL, NX, NZH, NCO = 8, 6, 4, 2, 2
AXES = ("y", "zl", "x", "zh", "co")
DP = ("y", "zl")
CTX = ("x", "zh", "co")
EPS = 1e-06
F32 = jnp.float32
BF16 = jnp.bfloat16


def gelu_slope(values):
    normal_cdf = 0.5 * (1.0 + lax.erf(values * 0.7071067811865476))
    density = jnp.exp(-0.5 * values * values) * 0.3989422804014327
    return normal_cdf + values * density


def params(mib=12):
    return pltpu.CompilerParams(vmem_limit_bytes=mib * 1024 * 1024)


def cost(flops=1):
    return pl.CostEstimate(flops=flops, bytes_accessed=1, transcendentals=0)


LONG = 20_000_000_000
ANYWHERE = pl.BlockSpec(memory_space=pl.ANY)
IN_VMEM = pl.BlockSpec(memory_space=pltpu.VMEM)
IN_SMEM = pl.BlockSpec(memory_space=pltpu.SMEM)


def swap(value, axis):
    return lax.ppermute(value, axis, [(0, 1), (1, 0)])


def hidden_kernel(core, own_w, got_w, own_t, got_t, out_ref):
    depth = own_t.shape[1]
    total = None
    for w_ref, t_ref in ((own_w, own_t), (got_w, got_t)):
        term = lax.dot_general(
            w_ref[...].reshape(-1, depth),
            t_ref[...],
            (((1,), (1,)), ((), ())),
            preferred_element_type=F32,
        )
        total = term if total is None else total + term
    out_ref[...] = total.astype(BF16).reshape(out_ref.shape)


def hidden_part(weights, tokens, core):
    rows, depth = weights[0].shape
    units = rows // (NX * NZH * NCO)
    count = tokens[0].shape[0]
    weights = [w.reshape(NX, NZH, NCO, units, depth) for w in weights]
    w_spec = pl.BlockSpec((1, NZH, 1, units, depth), lambda i, s: (i, 0, s[0], 0, 0))
    t_spec = pl.BlockSpec((count, depth), lambda i, s: (0, 0))
    return pl.pallas_call(
        hidden_kernel,
        grid_spec=pltpu.PrefetchScalarGridSpec(
            num_scalar_prefetch=1,
            grid=(NX,),
            in_specs=[w_spec, w_spec, t_spec, t_spec],
            out_specs=pl.BlockSpec((1, NZH, units, count), lambda i, s: (i, 0, 0, 0)),
        ),
        out_shape=jax.ShapeDtypeStruct((NX, NZH, units, count), BF16),
        compiler_params=params(52),
        cost_estimate=cost(),
        name="hidden_part",
    )(core, *weights, *tokens)


def total_of(ref, z):
    total = ref[0, z].astype(F32)
    for i in range(1, ref.shape[0]):
        total += ref[i, z].astype(F32)
    return total


def sum_kernel(place, v_ref, out_ref):
    out_ref[...] = total_of(v_ref, place[0]).astype(BF16)


def sum_parts(parts, place):
    return pl.pallas_call(
        sum_kernel,
        in_specs=[IN_SMEM, IN_VMEM],
        out_specs=IN_VMEM,
        out_shape=jax.ShapeDtypeStruct(parts.shape[2:], BF16),
        compiler_params=params(),
        cost_estimate=cost(),
        name="sum_parts",
    )(place, parts)


def wide_kernel(v_ref, out_ref):
    out_ref[...] = v_ref[...].astype(F32)


def widen(value):
    return pl.pallas_call(
        wide_kernel,
        out_shape=jax.ShapeDtypeStruct(value.shape, F32),
        compiler_params=params(),
        cost_estimate=cost(LONG),
        name="widen",
    )(value)


def act_kernel(place, v_ref, got_ref, slope_ref, pos_ref, out_ref):
    act = ((total_of(v_ref, place[0]) + got_ref[...]) * slope_ref[...]).astype(BF16)
    count = act.shape[1]
    pick = (lax.broadcasted_iota(jnp.int32, (count, count), 0) == pos_ref[...]).astype(F32)
    pick = pick.T.astype(BF16)
    moved = lax.dot_general(pick, act, (((1,), (1,)), ((), ())), preferred_element_type=F32)
    moved = moved.astype(BF16)
    own = out_ref.shape[3]
    for x in range(NX):
        for z in range(NZH):
            for c in range(NCO):
                first = ((x * NZH + z) * NCO + c) * own
                out_ref[x, c, z] = moved[first : first + own]


def act_rows(parts, got, slope, owner_pos, place):
    units, count = got.shape
    return pl.pallas_call(
        act_kernel,
        in_specs=[IN_SMEM] + [IN_VMEM] * 4,
        out_specs=IN_VMEM,
        out_shape=jax.ShapeDtypeStruct((NX, NCO, NZH, count // (NX * NCO * NZH), units), BF16),
        compiler_params=params(),
        cost_estimate=cost(),
        name="act_rows",
    )(place, parts, got, slope, owner_pos.reshape(1, count))


def merged_kernel(place, own_a, got_a, own_w, got_w, out_ref):
    depth = own_w.shape[0]
    total = None
    for a_ref, w_ref in ((own_a, own_w), (got_a, got_w)):
        term = lax.dot_general(
            a_ref[...].reshape(-1, depth),
            w_ref[...],
            (((1,), (0,)), ((), ())),
            preferred_element_type=F32,
        )
        total = term if total is None else total + term
    out_ref[...] = total.astype(BF16).reshape(out_ref.shape)


def merged_part(acts, weights, core):
    depth = acts[0].shape[-1]
    cols = weights[0].shape[1] // NCO
    steps = 2
    a_spec = pl.BlockSpec(acts[0].shape, lambda i, s: (0, 0, 0, 0, 0))
    w_spec = pl.BlockSpec((depth, cols // steps), lambda i, s: (0, s[0] * steps + i))
    shape = acts[0].shape[:-1]
    return pl.pallas_call(
        merged_kernel,
        grid_spec=pltpu.PrefetchScalarGridSpec(
            num_scalar_prefetch=1,
            grid=(steps,),
            in_specs=[a_spec, a_spec, w_spec, w_spec],
            out_specs=pl.BlockSpec(shape + (cols // steps,), lambda i, s: (0, 0, 0, 0, i)),
        ),
        out_shape=jax.ShapeDtypeStruct(shape + (cols,), BF16),
        compiler_params=params(52),
        cost_estimate=cost(),
        name="merged_part",
    )(core, *acts, *weights)


def halves_kernel(place, v_ref, out_ref):
    z = place[0]
    for c in range(NCO):
        total = v_ref[c, z].astype(F32)
        for x in range(1, NX):
            total += v_ref[NCO * x + c, z].astype(F32)
        out_ref[c] = total.astype(BF16)


def sum_halves(parts, place):
    return pl.pallas_call(
        halves_kernel,
        in_specs=[IN_SMEM, IN_VMEM],
        out_specs=IN_VMEM,
        out_shape=jax.ShapeDtypeStruct((NCO,) + parts.shape[2:], BF16),
        compiler_params=params(),
        cost_estimate=cost(),
        name="sum_halves",
    )(place, parts)


def pack_kernel(width, core, own_ref, got_ref, out_ref):
    half = out_ref.shape[2]
    for c, ref in ((core[0], own_ref), (1 - core[0], got_ref)):
        for p in range(half // width):
            cols = pl.ds(pl.multiple_of(core[0] * half + p * width, 128), width)
            normed, _ = norm_of(ref[:, cols].astype(F32))
            out_ref[c, :, p * width : (p + 1) * width] = normed.astype(BF16)


def pack_patches(own, got, core, width):
    rows, cols = own.shape
    return pl.pallas_call(
        functools.partial(pack_kernel, width),
        in_specs=[IN_SMEM, IN_VMEM, IN_VMEM],
        out_specs=IN_VMEM,
        out_shape=jax.ShapeDtypeStruct((NCO, rows, cols // NCO), BF16),
        compiler_params=params(),
        cost_estimate=cost(),
        name="pack_patches",
    )(core, own, got)


def norm_of(patch):
    inv_rms = lax.rsqrt(jnp.mean(patch * patch, axis=-1, keepdims=True) + EPS)
    return patch * inv_rms, inv_rms


def gain_kernel(place, grad_ref, *refs):
    out_ref = refs[-1]
    width = out_ref.shape[1]
    terms = jnp.zeros((1, width), F32)
    for shift, patch_ref in enumerate(refs[:-1]):
        x = lax.rem(place[0] + shift, NX)
        for k in range(NZH):
            z = place[1] if k == 0 else 1 - place[1]
            for c in range(NCO):
                for p in range(grad_ref.shape[4] // width):
                    cols = pl.ds(p * width, width)
                    normed = patch_ref[k, c, :, cols].astype(F32)
                    grad = grad_ref[x, c, z, :, cols].astype(F32)
                    terms += jnp.sum(grad * normed, axis=0, keepdims=True)
    out_ref[...] = terms


def gain_terms(grads, patches, place, width):
    return pl.pallas_call(
        gain_kernel,
        in_specs=[IN_SMEM] + [IN_VMEM] * (1 + NX),
        out_specs=IN_VMEM,
        out_shape=jax.ShapeDtypeStruct((1, width), F32),
        compiler_params=params(),
        cost_estimate=cost(LONG),
        name="gain_terms",
    )(place, grads, *patches)


def norm_kernel(place, v_ref, got_ref, patch_ref, gain_ref, out_ref):
    width = gain_ref.shape[1]
    gain = gain_ref[...]
    z = place[0]
    in_half = patch_ref.shape[1] // width // NCO
    for p in range(patch_ref.shape[1] // width):
        c, q = p // in_half, pl.ds(p % in_half * width, width)
        cols = pl.ds(p * width, width)
        owner = got_ref[c, :, q].astype(F32)
        for x in range(NX):
            owner += v_ref[NCO * x + c, z, :, q].astype(F32)
        normed, inv_rms = norm_of(patch_ref[:, cols].astype(F32))
        scaled = owner * gain
        inner = jnp.mean(scaled * normed, axis=-1, keepdims=True)
        out_ref[:, cols] = (inv_rms * (scaled - normed * inner)).astype(BF16)


def norm_part(parts, got, patch_in, norm_gain, place):
    return pl.pallas_call(
        norm_kernel,
        in_specs=[IN_SMEM] + [IN_VMEM] * 4,
        out_specs=IN_VMEM,
        out_shape=jax.ShapeDtypeStruct(patch_in.shape, BF16),
        compiler_params=params(),
        cost_estimate=cost(LONG),
        name="norm_part",
    )(place, parts, got, patch_in, norm_gain.reshape(1, -1))


def sum_over(terms, axes, count):
    rows = jnp.broadcast_to(terms[None], (count,) + terms.shape)
    return jnp.sum(lax.all_to_all(rows, axes, 0, 0, tiled=True), axis=0)


def local(grad_tokens, pre_act, w_fc1, w_fc2, patch_in, norm_gain, owner_pos):
    zh = lax.axis_index("zh").astype(jnp.int32)
    co = lax.axis_index("co").astype(jnp.int32)
    ctx = NX * NZH * NCO
    own, depth = grad_tokens.shape
    group = own * ctx
    slope = gelu_slope(pre_act.astype(F32))
    far_z, near_z, core = (1 - zh).reshape(1), zh.reshape(1), co.reshape(1)
    half = patch_in.shape[1] // NCO
    with jax.named_scope("tokens"):
        outgoing = grad_tokens.reshape(own, ctx, depth // ctx).transpose(1, 0, 2)
        tokens = lax.all_to_all(outgoing, CTX, 0, 0, tiled=True).reshape(group, depth // ctx)
        beside = swap(patch_in, "co")
        tokens, beside = lax.optimization_barrier((tokens, beside))
        tokens = (tokens, swap(tokens, "co"))
    with jax.named_scope("weights"):
        weights_2 = (w_fc2, swap(w_fc2, "co"))
        w_fc1_t = w_fc1.T

    with jax.named_scope("patches"):
        patches = pack_patches(patch_in, beside, core, norm_gain.shape[0])

    def tie(value, first):
        return lax.optimization_barrier((value, first))[0]

    with jax.named_scope("hidden"):
        sums = hidden_part(weights_2, tokens, core)
        parts = lax.all_to_all(sums, "x", 0, 0, tiled=True)
        ready = tie(patches, sums)
        weights_1 = (w_fc1_t, swap(w_fc1_t, "co"))
        beyond = swap(ready, "zh")
        far = sum_parts(parts, far_z)
        got = widen(swap(far, "zh"))
        patches = jnp.stack([tie(patches, far), beyond])
        around = [patches] + [
            lax.ppermute(patches, "x", [(i, (i - d) % NX) for i in range(NX)]) for d in (1, 2, 3)
        ]
    with jax.named_scope("merged"):
        act = act_rows(parts, got, slope, owner_pos, near_z)
        sums = merged_part((act, swap(act, "co")), weights_1, core)
        parts = lax.all_to_all(
            sums.reshape(NX * NCO, NZH * own, half), ("x", "co"), 0, 0, tiled=True
        ).reshape(NX * NCO, NZH, own, half)
        here = jnp.stack([lax.axis_index("x").astype(jnp.int32), zh])
        terms = gain_terms(sums, around, here, norm_gain.shape[0]).reshape(-1, 128)
        terms = lax.psum(terms, "y")
        parts, terms = lax.optimization_barrier((parts, terms))
        far = sum_halves(parts, far_z)
        got = swap(far, "zh")
    with jax.named_scope("gain"):
        terms = sum_over(tie(terms, far), ("zl", "zh"), NZL * NZH)
    with jax.named_scope("norm"):
        patch_grad = norm_part(parts, got, patch_in, norm_gain, near_z)
    with jax.named_scope("gain"):
        terms = sum_over(terms, ("x", "co"), NX * NCO)
        gain_grad = terms.reshape(-1) / (NY * NZL * ctx)
    return (patch_grad, gain_grad)


def solution(mesh):
    fine = Mesh(mesh.devices.reshape(NY, NZL, NX, NZH, NCO), AXES)
    return jax.shard_map(
        local,
        mesh=fine,
        in_specs=(
            P(DP + CTX, None),
            P(CTX, DP),
            P(None, CTX),
            P(None, CTX),
            P(DP + CTX, None),
            P(),
            P(DP),
        ),
        out_specs=(P(DP + CTX, None), P()),
        check_vma=False,
    )
```
